128 devices in a mesh: gx: 4 (over z), gy: 4 (over y), gz: 8 (over x, core).
Axes of the slice: x: 4, y: 4, z: 4, core: 2. Of those that a mesh axis runs over, the one named last changes fastest.
Arguments:
- intensity: float32 [32, 128, 1024], P('gx', 'gy', 'gz'), may hold values from -24 to 24
- seed_labels: int32 [32, 128, 1024], P('gx', 'gy', 'gz'), may hold values from -1 to 7, as said below
Outputs:
- solution: float32 [8, 32, 128, 1024], P(None, 'gx', 'gy', 'gz')
- residual: float32 [8, 32, 128, 1024], P(None, 'gx', 'gy', 'gz')
- direction: float32 [8, 32, 128, 1024], P(None, 'gx', 'gy', 'gz')
The draws below stay inside these ranges and needn't reach their ends.
Inputs may be any that keep to these rules, and one draw needn't show every extreme that they name: `seed_labels`: -1 marks an unseeded voxel, any other value is the voxel's seed label.
All inputs are finite; a program needn't handle non-finite values.
Results may differ from the reference program's by a relative error of at most 0.0003.
Values sent between devices are 32-bit elements; how exact they have to be, the bound alone decides.
No kernel may reach another device: no remote copies, remote signals or barrier semaphores. Data moves between devices by JAX's collectives and lax.ppermute only.
A program may use at most 128 MiB of HBM per device.

```python
import jax
import jax.numpy as jnp
from jax import lax

LABELS = 8
SWEEPS = 2
COARSE_SWEEPS = 6
NX = 32
NY = 128
NZ = 1024


def draw_intensity(key, part):
    noise_key = jax.random.fold_in(key, 23)
    shape = (NX, NY, NZ)
    pos_z = lax.broadcasted_iota(jnp.float32, shape, 2) / max(NZ - 1, 1)
    noise = jnp.clip(jax.random.normal(noise_key, shape, jnp.float32), -6.0, 6.0)
    contrast = 0.15 * jnp.exp(jnp.log(20.0) * pos_z)
    return (noise * contrast).astype(jnp.float32)


def draw_seed_labels(key, part):
    label_key, keep_key = jax.random.split(jax.random.fold_in(key, 11))
    shape = (NX, NY, NZ)
    label_ids = jax.random.randint(label_key, shape, 0, LABELS)
    pos_x = lax.broadcasted_iota(jnp.int32, shape, 0)
    pos_z = lax.broadcasted_iota(jnp.int32, shape, 2)
    limit = 1 + 15 * pos_x // (2 * max(NX - 1, 1)) + 15 * pos_z // (2 * max(NZ - 1, 1))
    chosen = jax.random.randint(keep_key, shape, 0, 64) < limit
    return jnp.where(chosen, label_ids, -1).astype(jnp.int32)


def setup_inputs(seed: int = 0) -> dict:
    arg_keys = jax.random.split(jax.random.key(seed), 3)
    return {
        "intensity": draw_intensity(jax.random.fold_in(arg_keys[2], 71), 0),
        "seed_labels": draw_seed_labels(jax.random.fold_in(arg_keys[2], 71), 0),
    }


BETA = 0.5
WFLOOR = 0.01
REACT = 0.01
PENALTY = 4.0
OMEGA = 0.8


def edge_weight(contrast):
    return jnp.exp(-BETA * contrast * contrast) + WFLOOR


def shift_lower(weights, axis_no):
    head = jnp.zeros_like(lax.slice_in_dim(weights, 0, 1, axis=axis_no))
    kept = lax.slice_in_dim(weights, 0, weights.shape[axis_no] - 1, axis=axis_no)
    return jnp.concatenate([head, kept], axis=axis_no)


def make_level(uppers, source):
    lowers = (shift_lower(uppers[0], 0), shift_lower(uppers[1], 1), shift_lower(uppers[2], 2))
    diagonal = source + uppers[0] + uppers[1] + uppers[2] + lowers[0] + lowers[1] + lowers[2]
    return (uppers, lowers, source, diagonal)


def neighbour_sum(padded, grid_level):
    uppers, lowers = grid_level[0], grid_level[1]
    summed = uppers[0] * padded[..., 2:, 1:-1, 1:-1] + lowers[0] * padded[..., :-2, 1:-1, 1:-1]
    summed = summed + uppers[1] * padded[..., 1:-1, 2:, 1:-1] + lowers[1] * padded[..., 1:-1, :-2, 1:-1]
    summed = summed + uppers[2] * padded[..., 1:-1, 1:-1, 2:] + lowers[2] * padded[..., 1:-1, 1:-1, :-2]
    return summed


def operate(vector, grid_level):
    return grid_level[3] * vector - neighbour_sum(jnp.pad(vector, 1), grid_level)


def fold_x(weights, offset):
    extent = weights.shape
    return weights[offset::2].reshape(extent[0] // 2, extent[1] // 2, 2, extent[2] // 2, 2).sum(axis=(2, 4))


def fold_y(weights, offset):
    extent = weights.shape
    return weights[:, offset::2].reshape(extent[0] // 2, 2, extent[1] // 2, extent[2] // 2, 2).sum(axis=(1, 4))


def fold_z(weights, offset):
    extent = weights.shape
    return weights[:, :, offset::2].reshape(extent[0] // 2, 2, extent[1] // 2, 2, extent[2] // 2).sum(axis=(1, 3))


def block_sum(source):
    extent = source.shape
    return source.reshape(extent[0] // 2, 2, extent[1] // 2, 2, extent[2] // 2, 2).sum(axis=(1, 3, 5))


def coarsen(grid_level):
    uppers, source = grid_level[0], grid_level[2]
    return make_level((fold_x(uppers[0], 1), fold_y(uppers[1], 1), fold_z(uppers[2], 1)), block_sum(source))


def prolong(vector):
    extent = vector.shape
    spread = jnp.broadcast_to(vector[:, None, :, None, :, None], (extent[0], 2, extent[1], 2, extent[2], 2))
    return spread.reshape(2 * extent[0], 2 * extent[1], 2 * extent[2])


def smooth(approx, target, grid_level):
    return approx + OMEGA * (target - operate(approx, grid_level)) / grid_level[3]


def relax_level(target, grid_level):
    approx = OMEGA * target / grid_level[3]
    for sweep_no in range(SWEEPS - 1):
        approx = smooth(approx, target, grid_level)
    return approx


def post_relax(approx, target, grid_level):
    for sweep_no in range(SWEEPS):
        approx = smooth(approx, target, grid_level)
    return approx


def vcycle(target, fine, middle, coarse):
    error_fine = relax_level(target, fine)
    target_mid = block_sum(target - operate(error_fine, fine))
    error_mid = relax_level(target_mid, middle)
    target_low = block_sum(target_mid - operate(error_mid, middle))
    error_low = OMEGA * target_low / coarse[3]
    for sweep_no in range(COARSE_SWEEPS - 1):
        error_low = smooth(error_low, target_low, coarse)
    error_mid = post_relax(error_mid + prolong(error_low), target_mid, middle)
    return post_relax(error_fine + prolong(error_mid), target, fine)


def reference(intensity, seed_labels):
    zero_x = jnp.zeros((1, NY, NZ), jnp.float32)
    zero_y = jnp.zeros((NX, 1, NZ), jnp.float32)
    zero_z = jnp.zeros((NX, NY, 1), jnp.float32)
    upper_x = jnp.concatenate([edge_weight(intensity[1:] - intensity[:-1]), zero_x], axis=0)
    upper_y = jnp.concatenate([edge_weight(intensity[:, 1:] - intensity[:, :-1]), zero_y], axis=1)
    upper_z = jnp.concatenate([edge_weight(intensity[:, :, 1:] - intensity[:, :, :-1]), zero_z], axis=2)
    source = REACT + PENALTY * (seed_labels >= 0).astype(jnp.float32)
    fine = make_level((upper_x, upper_y, upper_z), source)
    middle = coarsen(fine)
    coarse = coarsen(middle)

    def solve_label(label_id):
        right_side = PENALTY * (seed_labels == label_id).astype(jnp.float32)
        precond = vcycle(right_side, fine, middle, coarse)
        first_dot = jnp.sum(right_side * precond)
        image = operate(precond, fine)
        curvature = jnp.sum(precond * image)
        step_size = first_dot / curvature
        solution = step_size * precond
        residual = right_side - step_size * image
        precond_next = vcycle(residual, fine, middle, coarse)
        next_dot = jnp.sum(residual * precond_next)
        direction = precond_next + (next_dot / first_dot) * precond
        return (solution, residual, direction)

    solution, residual, direction = lax.map(solve_label, jnp.arange(LABELS, dtype=jnp.int32))
    return (solution, residual, direction)
```

```python
import functools

import jax
import jax.numpy as jnp
from jax import lax
from jax.experimental import pallas as pl
from jax.experimental.pallas import tpu as pltpu
from jax.sharding import PartitionSpec as P


LABELS = 8
BETA = 0.5
WFLOOR = 0.01
REACT = 0.01
PENALTY = 4.0
OMEGA = 0.8
KEEP = 1.0 - OMEGA
COARSE_SWEEPS = 6
VLIMIT = 40 * 1024 * 1024
F32 = jnp.float32


def lanes(v, shift):
    return pltpu.roll(v, shift % 128, 1)


def rows(v, shift):
    return pltpu.roll(v, shift % v.shape[0], 0)


def lane_id(shape):
    return lax.broadcasted_iota(jnp.int32, shape, 1)


def row_id(shape):
    return lax.broadcasted_iota(jnp.int32, shape, 0)


def neighbours(v_ref, uxs_ref, uy_ref, uz_ref, x, stride, ghost):
    if ghost:
        below, v, above = v_ref[x], v_ref[x + 1], v_ref[x + 2]
    else:
        last = v_ref.shape[0] - 1
        below, v, above = v_ref[jnp.maximum(x - 1, 0)], v_ref[x], v_ref[jnp.minimum(x + 1, last)]
    uy, uz = uy_ref[x], uz_ref[x]
    total = uxs_ref[x + 1] * above + uxs_ref[x] * below
    total = total + uy * lanes(v, -stride) + lanes(uy * v, stride)
    total = total + uz * rows(v, -1) + rows(uz * v, 1)
    return v, total


def diagonal(source, uxs_ref, uy_ref, uz_ref, x, stride):
    uy, uz = uy_ref[x], uz_ref[x]
    return source + uxs_ref[x + 1] + uxs_ref[x] + uy + lanes(uy, stride) + uz + rows(uz, 1)


def ghosts(v_ref, n):
    v_ref[0] = lanes(v_ref[n], 1)
    v_ref[n + 1] = lanes(v_ref[1], -1)


def halo_kernel(i_ref, s_ref, up_ref, dn_ref):
    lane = lane_id((32, 128))
    up = jnp.zeros((32, 128), F32)
    dn = jnp.zeros((32, 128), F32)
    for x in range(8):
        for side, v in ((0, i_ref[x]), (64, s_ref[x].astype(F32))):
            start = side + 8 * x
            here = (lane >= start) & (lane < start + 8)
            up = jnp.where(here, lanes(v, start - 120), up)
            dn = jnp.where(here, lanes(v, start), dn)
    up_ref[...] = up
    dn_ref[...] = dn


def pack_kernel(odd_ref, i_ref, s_ref, left_ref, right_ref, oi_ref, os_ref):
    odd = odd_ref[0]
    lane = lane_id((32, 128))
    low = lane < 64
    left, right = left_ref[...], right_ref[...]
    for which, (v_ref, o_ref) in enumerate(((i_ref, oi_ref), (s_ref, os_ref))):
        parts = ([], [])
        for x in range(4):
            a, b = v_ref[x].astype(F32), v_ref[x + 4].astype(F32)
            parts[0].append(jnp.where(low, a, lanes(b, 64)))
            parts[1].append(jnp.where(low, lanes(a, 64), b))
        from_left = left if which == 0 else lanes(left, 64)
        from_right = lanes(right, 64) if which == 0 else right
        own_above, own_below = from_left, from_right
        for x in range(8):
            v = v_ref[x].astype(F32)
            start = 64 + 8 * x
            own_above = jnp.where((lane >= start) & (lane < start + 8), lanes(v, start - 64), own_above)
            start = 8 * x
            own_below = jnp.where((lane >= start) & (lane < start + 8), lanes(v, start - 56), own_below)
        parts[0].append(own_above)
        parts[1].append(own_below)
        for label in range(LABELS):
            for half in range(2):
                slot = 2 * label + jnp.bitwise_xor(odd, half)
                for k in range(5):
                    o_ref[slot, k] = parts[half][k]


def assemble(r_ref, v_ref):
    for gx in range(4):
        for k in range(4):
            block = r_ref[4 * gx : 4 * gx + 4, k].reshape(128, 128)
            turned = block.T
            v_ref[8 * gx + k, 8:72] = turned[:64]
            v_ref[8 * gx + k + 4, 8:72] = turned[64:]
        turned = r_ref[4 * gx : 4 * gx + 4, 4].reshape(128, 128).T
        for x in range(8):
            v_ref[8 * gx + x, 0:8] = turned[8 * x : 8 * x + 8]
            v_ref[8 * gx + x, 72:80] = turned[64 + 8 * x : 72 + 8 * x]


def spread(v_ref, o_ref):
    for gx in range(4):
        for k in range(4):
            a, b = v_ref[8 * gx + k, 8:72], v_ref[8 * gx + k + 4, 8:72]
            o_ref[4 * gx : 4 * gx + 4, k] = jnp.concatenate([a, b], axis=0).T.reshape(4, 32, 128)


def plane_pair(v_ref, x, both_x, upper_z):
    total = v_ref[x, pl.ds(9, 32, stride=2), :]
    if not upper_z:
        total = total + v_ref[x, pl.ds(8, 32, stride=2), :]
    if both_x:
        total = total + plane_pair(v_ref, x + 1, False, upper_z)
    return total


def pack_pair(a, b):
    even = lane_id(a.shape) % 2 == 0
    return jnp.where(even, a + lanes(a, -1), b + lanes(b, 1))


def restrict_fine(v_ref, o_ref, slot):
    def body(x, c):
        a = plane_pair(v_ref, 2 * x, True, False)
        b = plane_pair(v_ref, 2 * x + 16, True, False)
        o_ref[slot, x] = pack_pair(a, b)
        return c

    lax.fori_loop(0, 8, body, 0)


def edge_weight(contrast):
    return jnp.exp(-BETA * contrast * contrast) + WFLOOR


def weights_kernel(zb_ref, r_ref, uxs_ref, uy_ref, uz_ref, w1_ref, v_ref):
    assemble(r_ref, v_ref)
    lane = lane_id((80, 128))
    place = row_id((80, 128)) + (zb_ref[0] - 8)
    cut = (place == -1) | (place == 1023)
    uxs_ref[0] = jnp.zeros((80, 128), F32)

    def body(x, c):
        v = v_ref[x]
        above = v_ref[jnp.minimum(x + 1, 31)]
        uxs_ref[x + 1] = jnp.where(x == 31, 0.0, edge_weight(above - v))
        uy_ref[x] = jnp.where(lane == 127, 0.0, edge_weight(lanes(v, -1) - v))
        uz_ref[x] = jnp.where(cut, 0.0, edge_weight(rows(v, -1) - v))
        return c

    lax.fori_loop(0, 32, body, 0)
    even = lane_id((32, 128)) % 2 == 0

    def coarse(x, c):
        w1_ref[0, x] = pack_pair(
            plane_pair(uxs_ref, 2 * x + 2, False, False), plane_pair(uxs_ref, 2 * x + 18, False, False)
        )
        a, b = plane_pair(uy_ref, 2 * x, True, False), plane_pair(uy_ref, 2 * x + 16, True, False)
        w1_ref[1, x] = jnp.where(even, lanes(a, -1), b)
        w1_ref[2, x] = pack_pair(
            plane_pair(uz_ref, 2 * x, True, True), plane_pair(uz_ref, 2 * x + 16, True, True)
        )
        return c

    lax.fori_loop(0, 8, coarse, 0)


def pre_relax(f_ref, g_ref, e_ref, t_ref, level, stride=1):
    uxs_ref, uy_ref, uz_ref, d_ref, di_ref = level

    def sweep(x, c):
        v, total = neighbours(g_ref, uxs_ref, uy_ref, uz_ref, x, 1, False)
        e_ref[x] = KEEP * v + di_ref[x] * (f_ref[x] + total)
        return c

    lax.fori_loop(0, 32, sweep, 0)

    def rest(x, c):
        v, total = neighbours(e_ref, uxs_ref, uy_ref, uz_ref, x, 1, False)
        t_ref[x] = f_ref[x] - d_ref[x] * v + total
        return c

    lax.fori_loop(0, 32, rest, 0)


def first_kernel(lab_ref, r_ref, uxs_ref, uy_ref, uz_ref, d_ref, di_ref, f_ref, e_ref, l1_ref, s_ref, g_ref):
    assemble(r_ref, s_ref)
    label = lab_ref[0].astype(F32)

    def setup(x, c):
        seed = s_ref[x]
        f = jnp.where(seed == label, PENALTY, 0.0)
        source = jnp.where(seed >= 0.0, REACT + PENALTY, REACT)
        d = diagonal(source, uxs_ref, uy_ref, uz_ref, x, 1)
        di = OMEGA / d
        s_ref[x] = source
        f_ref[x] = f
        d_ref[x] = d
        di_ref[x] = di
        g_ref[x] = di * f
        return c

    lax.fori_loop(0, 32, setup, 0)
    restrict_fine(s_ref, l1_ref, 1)
    pre_relax(f_ref, g_ref, e_ref, s_ref, (uxs_ref, uy_ref, uz_ref, d_ref, di_ref))
    restrict_fine(s_ref, l1_ref, 0)


def add_coarse(e_ref, c_ref, o_ref, p_ref):
    def body(x, c):
        v = c_ref[x]
        even = lane_id((40, 128)) % 2 == 0
        for part in range(2):
            if part == 0:
                w = jnp.where(even, v, 0.0)
                w = w + lanes(w, 1)
            else:
                w = jnp.where(even, 0.0, v)
                w = w + lanes(w, -1)
            p_ref[pl.ds(0, 40, stride=2), :] = w
            p_ref[pl.ds(1, 40, stride=2), :] = w
            wide = p_ref[...]
            at = 2 * x + 16 * part
            o_ref[at] = e_ref[at] + wide
            o_ref[at + 1] = e_ref[at + 1] + wide
        return c

    lax.fori_loop(0, 8, body, 0)


def post_relax(f_ref, a_ref, b_ref, level):
    uxs_ref, uy_ref, uz_ref, di_ref = level
    for src, dst in ((a_ref, b_ref), (b_ref, a_ref)):

        def sweep(x, c):
            v, total = neighbours(src, uxs_ref, uy_ref, uz_ref, x, 1, False)
            dst[x] = KEEP * v + di_ref[x] * (f_ref[x] + total)
            return c

        lax.fori_loop(0, 32, sweep, 0)


def dot_core(a_ref, b_ref):
    def body(x, c):
        p = a_ref[x, 8:72] * b_ref[x, 8:72]
        return c + p

    return jnp.sum(lax.fori_loop(0, 32, body, jnp.zeros((64, 128), F32)))


def middle_kernel(
    c_ref, uxs_ref, uy_ref, uz_ref, d_ref, di_ref, f_ref, e_ref,
    zo_ref, qo_ref, q_ref, e2_ref, l1_ref, dots_ref, a_ref, b_ref, p_ref,
):
    add_coarse(e_ref, c_ref, a_ref, p_ref)
    post_relax(f_ref, a_ref, b_ref, (uxs_ref, uy_ref, uz_ref, di_ref))

    def image(x, c):
        v, total = neighbours(a_ref, uxs_ref, uy_ref, uz_ref, x, 1, False)
        q = d_ref[x] * v - total
        q_ref[x] = q
        b_ref[x] = di_ref[x] * q
        return c

    lax.fori_loop(0, 32, image, 0)
    spread(a_ref, zo_ref)
    spread(q_ref, qo_ref)
    rz = dot_core(f_ref, a_ref)
    pq = dot_core(a_ref, q_ref)
    row = row_id((8, 128))
    dots_ref[...] = jnp.where(row == 0, rz, pq)
    pre_relax(q_ref, b_ref, e2_ref, a_ref, (uxs_ref, uy_ref, uz_ref, d_ref, di_ref))
    restrict_fine(a_ref, l1_ref, 0)


def last_kernel(
    c_ref, uxs_ref, uy_ref, uz_ref, di_ref, f_ref, q_ref, e_ref, dots_ref, wo_ref, t_ref, a_ref, b_ref, p_ref
):
    add_coarse(e_ref, c_ref, a_ref, p_ref)
    post_relax(q_ref, a_ref, b_ref, (uxs_ref, uy_ref, uz_ref, di_ref))
    spread(a_ref, wo_ref)
    fw = dot_core(f_ref, a_ref)
    qw = dot_core(q_ref, a_ref)
    lane = lane_id((1, 128))
    line = jnp.where(lane == 0, dots_ref[0:1, :], dots_ref[1:2, :])
    line = jnp.where(lane == 2, fw, jnp.where(lane == 3, qw, line))
    t_ref[...] = jnp.broadcast_to(line, (128, 128))


def frame1(o_ref, core, left, right, at):
    for x in range(8):
        o_ref[x + at, 0:24] = left(x)
        o_ref[x + at, 24:56] = core(x)
        o_ref[x + at, 56:80] = right(x)


def pair1(v_ref, x, both_x, upper_z):
    total = v_ref[x, pl.ds(1, 40, stride=2), :]
    if not upper_z:
        total = total + v_ref[x, pl.ds(0, 40, stride=2), :]
    if both_x:
        total = total + pair1(v_ref, x + 1, False, upper_z)
    return total


def coarse_kernel(
    w_ref, wl_ref, wr_ref, s_ref, sl_ref, sr_ref, f_ref, fl_ref, fr_ref, o_ref,
    ux1, uy1, uz1, f1, d1, di1, v1, v1b, t1, ux2, uy2, uz2, f2, di2, v2, v2b, p_ref,
):
    for k, (dst, at) in enumerate(((ux1, 1), (uy1, 0), (uz1, 0))):
        frame1(dst, lambda x: w_ref[k, x], lambda x: wl_ref[k, x], lambda x: wr_ref[k, x], at)
    frame1(f1, lambda x: f_ref[0, x], lambda x: fl_ref[0, x], lambda x: fr_ref[0, x], 0)
    frame1(t1, lambda x: s_ref[0, x], lambda x: sl_ref[0, x], lambda x: sr_ref[0, x], 0)
    ux1[0] = lanes(ux1[8], 1)

    valid = lane_id((40, 128)) % 4 < 2

    def fold(v):
        return jnp.where(valid, v, 0.0)

    for x in range(4):
        a = pair1(ux1, 2 * x + 2, False, False)
        ux2[x + 1] = fold(a + lanes(a, -2))
        uy2[x] = fold(lanes(pair1(uy1, 2 * x, True, False), -2))
        a = pair1(uz1, 2 * x, True, True)
        uz2[x] = fold(a + lanes(a, -2))
    ux2[0] = lanes(ux2[4], 1)
    for x in range(4):
        a = pair1(t1, 2 * x, True, False)
        d = diagonal(fold(a + lanes(a, -2)), ux2, uy2, uz2, x, 4)
        di2[x] = jnp.where(d > 0.0, OMEGA / d, 0.0)

    def setup(x, c):
        d = diagonal(t1[x], ux1, uy1, uz1, x, 2)
        di = jnp.where(d > 0.0, OMEGA / d, 0.0)
        d1[x] = d
        di1[x] = di
        v1[x + 1] = di * f1[x]
        return c

    lax.fori_loop(0, 8, setup, 0)

    def relax1(src, dst):
        ghosts(src, 8)

        def sweep(x, c):
            v, total = neighbours(src, ux1, uy1, uz1, x, 2, True)
            dst[x + 1] = KEEP * v + di1[x] * (f1[x] + total)
            return c

        lax.fori_loop(0, 8, sweep, 0)

    relax1(v1, v1b)
    ghosts(v1b, 8)

    def rest(x, c):
        v, total = neighbours(v1b, ux1, uy1, uz1, x, 2, True)
        t1[x] = f1[x] - d1[x] * v + total
        return c

    lax.fori_loop(0, 8, rest, 0)

    for x in range(4):
        a = pair1(t1, 2 * x, True, False)
        f2[x] = fold(a + lanes(a, -2))
        v2[x + 1] = di2[x] * f2[x]
    src, dst = v2, v2b
    for _ in range(COARSE_SWEEPS - 1):
        ghosts(src, 4)
        for x in range(4):
            v, total = neighbours(src, ux2, uy2, uz2, x, 4, True)
            dst[x + 1] = KEEP * v + di2[x] * (f2[x] + total)
        src, dst = dst, src

    for x in range(4):
        w = src[x + 1]
        w = w + lanes(w, 2)
        p_ref[pl.ds(0, 40, stride=2), :] = w
        p_ref[pl.ds(1, 40, stride=2), :] = w
        wide = p_ref[...]
        v1b[2 * x + 1] = v1b[2 * x + 1] + wide
        v1b[2 * x + 2] = v1b[2 * x + 2] + wide
    relax1(v1b, v1)
    relax1(v1, v1b)
    for x in range(8):
        o_ref[x] = v1b[x + 1, 20:60]


def output_kernel(odd_ref, sc_ref, seed_ref, z_ref, q_ref, w_ref, sol_ref, res_ref, dir_ref):
    label = pl.program_id(0)
    odd = odd_ref[0]
    step, beta = sc_ref[0, label], sc_ref[1, label]
    low = lane_id((32, 128)) < 64
    for x in range(4):
        pair = []
        for ref in (z_ref, q_ref, w_ref):
            a, b = ref[odd, x], ref[1 - odd, x]
            pair.append((jnp.where(low, a, lanes(b, 64)), jnp.where(low, lanes(a, 64), b)))
        for k in range(2):
            z, q, w = pair[0][k], pair[1][k], pair[2][k]
            at = x + 4 * k
            f = jnp.where(seed_ref[at] == label, PENALTY, 0.0)
            sol_ref[0, at] = step * z
            res_ref[0, at] = f - step * q
            dir_ref[0, at] = (1.0 + beta) * z - step * w


def sds(*shape):
    return jax.ShapeDtypeStruct(shape, F32)


def call(kernel, out, args, smem=0, scratch=(), cost=1000000, name=None):
    vmem, scalar = pl.BlockSpec(memory_space=pltpu.VMEM), pl.BlockSpec(memory_space=pltpu.SMEM)
    return pl.pallas_call(
        kernel,
        out_shape=out,
        in_specs=[scalar] * smem + [vmem] * (len(args) - smem),
        out_specs=jax.tree.map(lambda _: vmem, out),
        scratch_shapes=[pltpu.VMEM(s, F32) for s in scratch],
        compiler_params=pltpu.CompilerParams(vmem_limit_bytes=VLIMIT),
        cost_estimate=pl.CostEstimate(flops=cost, bytes_accessed=cost, transcendentals=0),
        name=name,
    )(*args)


FINE = (32, 80, 128)


def z_chain():
    def at(label, gz, half):
        return (2 * label + (half ^ (gz & 1))) * 8 + gz

    pairs = []
    for label in range(LABELS):
        for gz in range(8):
            pairs.append((at(label, gz, 0), at(label, gz, 1)))
            if gz < 7:
                pairs.append((at(label, gz, 1), at(label, gz + 1, 0)))
    return pairs


def swap_planes(v):
    every = ("gx", "gy", "gz")
    up = z_chain()
    down = [(b, a) for a, b in up]
    return lax.ppermute(v[:, :, 8:32], every, up), lax.ppermute(v[:, :, 0:24], every, down)


def local(intensity, seed_labels):
    gx, gy, gz = lax.axis_index("gx"), lax.axis_index("gy"), lax.axis_index("gz")
    group = ("gx", "gy")
    odd = (gz & 1).reshape(1)
    half = (gy ^ gz) & 1
    label = ((4 * gx + gy) // 2).reshape(1)
    z_base = (128 * gz + 64 * half).reshape(1)

    up, dn = call(halo_kernel, [sds(32, 128), sds(32, 128)], (intensity, seed_labels), name="halo")
    chain = [(i, i + 1) for i in range(7)]
    left = lax.ppermute(up, "gz", chain)
    right = lax.ppermute(dn, "gz", [(b, a) for a, b in chain])
    pi, ps = call(
        pack_kernel, [sds(16, 5, 32, 128)] * 2, (odd, intensity, seed_labels, left, right), smem=1, name="pack"
    )
    ri = lax.all_to_all(pi, group, 0, 0, tiled=True)
    rs = lax.all_to_all(ps, group, 0, 0, tiled=True)
    uxs, uy, uz, w1 = call(
        weights_kernel,
        [sds(33, 80, 128), sds(*FINE), sds(*FINE), sds(3, 8, 32, 128)],
        (z_base, ri),
        smem=1,
        scratch=[FINE],
        name="weights",
    )
    wl, wr = swap_planes(w1)
    d, di, f, e, l1 = call(
        first_kernel,
        [sds(*FINE)] * 4 + [sds(2, 8, 32, 128)],
        (label, rs, uxs, uy, uz),
        smem=1,
        scratch=[FINE, FINE],
        name="first",
    )
    ll, lr = swap_planes(l1)

    def coarse(f1, fl, fr):
        big, small = (8, 80, 128), (4, 40, 128)
        return call(
            coarse_kernel,
            [sds(8, 40, 128)],
            (w1, wl, wr, l1[1:2], ll[1:2], lr[1:2], f1, fl, fr),
            scratch=[(9, 80, 128), big, big, big, big, big, (10, 80, 128), (10, 80, 128), big]
            + [(5, 40, 128), small, small, small, small, (6, 40, 128), (6, 40, 128), (80, 128)],
            name="coarse",
        )[0]

    c1 = coarse(l1[0:1], ll[0:1], lr[0:1])
    zo, qo, q, e2, m1, dots = call(
        middle_kernel,
        [sds(16, 4, 32, 128)] * 2 + [sds(*FINE)] * 2 + [sds(1, 8, 32, 128), sds(8, 128)],
        (c1, uxs, uy, uz, d, di, f, e),
        scratch=[FINE, FINE, (80, 128)],
        name="middle",
    )
    ml, mr = swap_planes(m1)
    zr = lax.all_to_all(zo, group, 0, 0, tiled=True)
    qr = lax.all_to_all(qo, group, 0, 0, tiled=True)
    c2 = coarse(m1, ml, mr)
    wo, tiny = call(
        last_kernel,
        [sds(16, 4, 32, 128), sds(128, 128)],
        (c2, uxs, uy, uz, di, f, q, e2, dots),
        scratch=[FINE, FINE, (80, 128)],
        name="last",
    )
    sums = lax.all_to_all(tiny, ("gx", "gy", "gz"), 0, 0, tiled=True)
    wr_ = lax.all_to_all(wo, group, 0, 0, tiled=True)
    sums = sums.reshape(LABELS, 16, 128)[:, :, :4].sum(axis=1)
    rz, pq, fw, qw = sums[:, 0], sums[:, 1], sums[:, 2], sums[:, 3]
    step = rz / pq
    beta = step * (step * qw - fw) / rz
    scal = jnp.stack([step, beta])

    block = pl.BlockSpec((2, 4, 32, 128), lambda i: (i, 0, 0, 0))
    smem = pl.BlockSpec(memory_space=pltpu.SMEM)
    return tuple(
        pl.pallas_call(
            output_kernel,
            grid=(LABELS,),
            out_shape=[sds(8, 8, 32, 128)] * 3,
            in_specs=[smem, smem, pl.BlockSpec((8, 32, 128), lambda i: (0, 0, 0)), block, block, block],
            out_specs=[pl.BlockSpec((1, 8, 32, 128), lambda i: (i, 0, 0, 0))] * 3,
            compiler_params=pltpu.CompilerParams(vmem_limit_bytes=VLIMIT),
            name="output",
        )(odd, scal, seed_labels, zr, qr, wr_)
    )


def solution(mesh):
    placed = (P("gx", "gy", "gz"), P("gx", "gy", "gz"))
    return jax.shard_map(
        local,
        mesh=mesh,
        in_specs=placed,
        out_specs=(P(None, "gx", "gy", "gz"), P(None, "gx", "gy", "gz"), P(None, "gx", "gy", "gz")),
        check_vma=False,
    )
```

```python
import functools

import jax
import jax.numpy as jnp
from jax import lax
from jax.experimental import pallas as pl
from jax.experimental.pallas import tpu as pltpu
from jax.sharding import PartitionSpec as P


LABELS = 8
BETA = 0.5
WFLOOR = 0.01
REACT = 0.01
PENALTY = 4.0
OMEGA = 0.8
KEEP = 1.0 - OMEGA
COARSE_SWEEPS = 6
VLIMIT = 44 * 1024 * 1024
F32 = jnp.float32


def lanes(v, shift):
    return pltpu.roll(v, shift % 128, 1)


def rows(v, shift):
    return pltpu.roll(v, shift % v.shape[0], 0)


def loop(n, body, group=8):
    def step(i, c):
        for k in range(group):
            body(group * i + k)
        return c

    if n == group:
        step(0, 0)
    else:
        lax.fori_loop(0, n // group, step, 0)


class Copies:
    def __init__(self, sems):
        self.sems, self.used, self.open = sems, 0, []

    def start(self, src, dst):
        copy = pltpu.make_async_copy(src, dst, self.sems.at[self.used])
        copy.start()
        self.used += 1
        self.open.append(copy)
        return copy

    def finish(self):
        for copy in self.open:
            copy.wait()
        self.open = []


def lane_id(shape):
    return lax.broadcasted_iota(jnp.int32, shape, 1)


def row_id(shape):
    return lax.broadcasted_iota(jnp.int32, shape, 0)


def neighbours(v_ref, uxs_ref, uy_ref, uz_ref, x, stride, ghost):
    if ghost:
        below, v, above = v_ref[x], v_ref[x + 1], v_ref[x + 2]
    else:
        last = v_ref.shape[0] - 1
        below, v, above = v_ref[jnp.maximum(x - 1, 0)], v_ref[x], v_ref[jnp.minimum(x + 1, last)]
    uy, uz = uy_ref[x], uz_ref[x]
    total = uxs_ref[x + 1] * above + uxs_ref[x] * below
    total = total + uy * lanes(v, -stride) + lanes(uy * v, stride)
    total = total + uz * rows(v, -1) + rows(uz * v, 1)
    return v, total


def diagonal(source, uxs_ref, uy_ref, uz_ref, x, stride):
    uy, uz = uy_ref[x], uz_ref[x]
    return source + uxs_ref[x + 1] + uxs_ref[x] + uy + lanes(uy, stride) + uz + rows(uz, 1)


def ghosts(v_ref, n):
    v_ref[0] = lanes(v_ref[n], 1)
    v_ref[n + 1] = lanes(v_ref[1], -1)


def pack_kernel(odd_ref, i_ref, s_ref, o_ref):
    odd = odd_ref[0]
    low = lane_id((32, 128)) < 64
    for field, v_ref in enumerate((i_ref, s_ref)):
        parts = ([], [])
        for x in range(4):
            a, b = v_ref[x].astype(F32), v_ref[x + 4].astype(F32)
            parts[0].append(jnp.where(low, a, lanes(b, 64)))
            parts[1].append(jnp.where(low, lanes(a, 64), b))
        for label in range(LABELS):
            for half in range(2):
                slot = 2 * label + jnp.bitwise_xor(odd, half)
                for k in range(4):
                    o_ref[slot, 4 * field + k] = parts[half][k]


def assemble_kernel(r_ref, core_ref, first_ref, last_ref):
    for gx in range(4):
        for k in range(8):
            turned = r_ref[4 * gx : 4 * gx + 4, k].reshape(128, 128).T
            for part in range(2):
                x = 32 * (k // 4) + 8 * gx + k % 4 + 4 * part
                core_ref[x] = turned[64 * part : 64 * part + 64]
                first_ref[x] = turned[64 * part : 64 * part + 8]
                last_ref[x] = turned[64 * part + 56 : 64 * part + 64]


def spread(v_ref, o_ref, field, copies, out_ref):
    for gx in range(4):
        for k in range(4):
            a, b = v_ref[8 * gx + k, 8:72], v_ref[8 * gx + k + 4, 8:72]
            turned = jnp.concatenate([a, b], axis=0).T.reshape(4, 32, 128)
            o_ref[4 * gx : 4 * gx + 4, 32 * (4 * field + k) : 32 * (4 * field + k + 1)] = turned
        part = (pl.ds(4 * gx, 4), pl.ds(128 * field, 128))
        copies.start(o_ref.at[part], out_ref.at[part])


def plane_pair(v_ref, x, both_x, upper_z):
    total = v_ref[x, pl.ds(9, 32, stride=2), :]
    if not upper_z:
        total = total + v_ref[x, pl.ds(8, 32, stride=2), :]
    if both_x:
        total = total + plane_pair(v_ref, x + 1, False, upper_z)
    return total


def pack_pair(a, b):
    even = lane_id(a.shape) % 2 == 0
    return jnp.where(even, a + lanes(a, -1), b + lanes(b, 1))


def restrict_fine(v_ref, o_ref, slot):
    def body(x):
        a = plane_pair(v_ref, 2 * x, True, False)
        b = plane_pair(v_ref, 2 * x + 16, True, False)
        o_ref[slot, x] = pack_pair(a, b)

    loop(8, body)


def edge_weight(contrast):
    return jnp.exp(-BETA * contrast * contrast) + WFLOOR


def pre_relax(f_ref, g_ref, e_ref, t_ref, level, then):
    uxs_ref, uy_ref, uz_ref, d_ref, di_ref = level

    def sweep(x):
        v, total = neighbours(g_ref, uxs_ref, uy_ref, uz_ref, x, 1, False)
        e_ref[x] = KEEP * v + di_ref[x] * (f_ref[x] + total)

    loop(32, sweep)
    then()

    def rest(x):
        v, total = neighbours(e_ref, uxs_ref, uy_ref, uz_ref, x, 1, False)
        t_ref[x] = f_ref[x] - d_ref[x] * v + total

    loop(32, rest)


def first_kernel(
    zb_ref, lab_ref, core_hbm, left_hbm, right_hbm,
    uxs_hbm, uy_hbm, uz_hbm, d_hbm, di_hbm, f_hbm, e_hbm, l1_ref,
    uxs_ref, uy_ref, uz_ref, d_ref, di_ref, f_ref, e_ref, v_ref, s_ref, sems,
):
    copies = Copies(sems)
    for base, dst in ((0, v_ref), (32, s_ref)):
        for src, at, n in ((left_hbm, 0, 8), (core_hbm, 8, 64), (right_hbm, 72, 8)):
            copies.start(src.at[pl.ds(base, 32)], dst.at[:, pl.ds(at, n)])
    arrived, copies.open = copies.open, []
    for copy in arrived[:3]:
        copy.wait()
    lane = lane_id((80, 128))
    place = row_id((80, 128)) + (zb_ref[0] - 8)
    cut = (place == -1) | (place == 1023)
    uxs_ref[0] = jnp.zeros((80, 128), F32)

    def body(x):
        v = v_ref[x]
        above = v_ref[jnp.minimum(x + 1, 31)]
        uxs_ref[x + 1] = jnp.where(x == 31, 0.0, edge_weight(above - v))
        uy_ref[x] = jnp.where(lane == 127, 0.0, edge_weight(lanes(v, -1) - v))
        uz_ref[x] = jnp.where(cut, 0.0, edge_weight(rows(v, -1) - v))

    loop(32, body, 4)
    even = lane_id((32, 128)) % 2 == 0

    def coarse(x):
        l1_ref[2, x] = pack_pair(
            plane_pair(uxs_ref, 2 * x + 2, False, False), plane_pair(uxs_ref, 2 * x + 18, False, False)
        )
        a, b = plane_pair(uy_ref, 2 * x, True, False), plane_pair(uy_ref, 2 * x + 16, True, False)
        l1_ref[3, x] = jnp.where(even, lanes(a, -1), b)
        l1_ref[4, x] = pack_pair(
            plane_pair(uz_ref, 2 * x, True, True), plane_pair(uz_ref, 2 * x + 16, True, True)
        )

    loop(8, coarse)
    copies.start(uxs_ref, uxs_hbm)
    copies.start(uy_ref, uy_hbm)
    copies.start(uz_ref, uz_hbm)
    for copy in arrived[3:]:
        copy.wait()
    label = lab_ref[0].astype(F32)

    def setup(x):
        seed = s_ref[x]
        f = jnp.where(seed == label, PENALTY, 0.0)
        source = jnp.where(seed >= 0.0, REACT + PENALTY, REACT)
        d = diagonal(source, uxs_ref, uy_ref, uz_ref, x, 1)
        di = OMEGA / d
        s_ref[x] = source
        f_ref[x] = f
        d_ref[x] = d
        di_ref[x] = di
        v_ref[x] = di * f

    loop(32, setup)
    copies.start(d_ref, d_hbm)
    copies.start(di_ref, di_hbm)
    copies.start(f_ref, f_hbm)
    restrict_fine(s_ref, l1_ref, 1)
    pre_relax(f_ref, v_ref, e_ref, s_ref, (uxs_ref, uy_ref, uz_ref, d_ref, di_ref), lambda: copies.start(e_ref, e_hbm))
    restrict_fine(s_ref, l1_ref, 0)
    copies.finish()


def add_coarse(e_ref, c_ref, o_ref, p_ref):
    even = lane_id((40, 128)) % 2 == 0

    def body(x):
        v = c_ref[x]
        for part in range(2):
            if part == 0:
                w = jnp.where(even, v, 0.0)
                w = w + lanes(w, 1)
            else:
                w = jnp.where(even, 0.0, v)
                w = w + lanes(w, -1)
            at = 2 * x + 16 * part
            slot = x % 4 + 4 * part
            p_ref[slot, pl.ds(0, 40, stride=2), :] = w
            p_ref[slot, pl.ds(1, 40, stride=2), :] = w
            wide = p_ref[slot]
            o_ref[at] = e_ref[at] + wide
            o_ref[at + 1] = e_ref[at + 1] + wide

    loop(8, body)


def post_relax(f_ref, a_ref, b_ref, level):
    uxs_ref, uy_ref, uz_ref, di_ref = level
    for src, dst in ((a_ref, b_ref), (b_ref, a_ref)):

        def sweep(x):
            v, total = neighbours(src, uxs_ref, uy_ref, uz_ref, x, 1, False)
            dst[x] = KEEP * v + di_ref[x] * (f_ref[x] + total)

        loop(32, sweep)


def dot_core(a_ref, b_ref, c_ref=None):
    def body(i, total):
        for k in range(4):
            b = b_ref[4 * i + k, 8:72]
            if c_ref is not None:
                b = b + c_ref[4 * i + k, 8:72]
            total = total + a_ref[4 * i + k, 8:72] * b
        return total

    return jnp.sum(lax.fori_loop(0, 8, body, jnp.zeros((64, 128), F32)))


def middle_kernel(
    l1, ll, lr, f1, fl, fr, uxs_hbm, uy_hbm, uz_hbm, d_hbm, di_hbm, f_hbm, e_hbm,
    zq_hbm, q_hbm, e2_hbm, m1_ref, dots_ref,
    uxs_ref, uy_ref, uz_ref, d_ref, di_ref, f_ref, e_ref, zq_ref, q_ref, a_ref, b_ref, p_ref, c_ref, *rest,
):
    copies = Copies(rest[-1])
    load1(copies, (l1, ll, lr), (f1, fl, fr), rest)
    small, copies.open = copies.open, []
    for src, dst in ((e_hbm, e_ref), (uxs_hbm, uxs_ref), (uy_hbm, uy_ref), (uz_hbm, uz_ref), (di_hbm, di_ref),
                     (f_hbm, f_ref), (d_hbm, d_ref)):
        copies.start(src, dst)
    for copy in small:
        copy.wait()
    coarse_solve(c_ref, *rest[:-1])
    copies.finish()
    add_coarse(e_ref, c_ref, a_ref, p_ref)
    post_relax(f_ref, a_ref, b_ref, (uxs_ref, uy_ref, uz_ref, di_ref))
    spread(a_ref, zq_ref, 0, copies, zq_hbm)

    def image(x):
        v, total = neighbours(a_ref, uxs_ref, uy_ref, uz_ref, x, 1, False)
        q = d_ref[x] * v - total
        q_ref[x] = q
        b_ref[x] = di_ref[x] * q

    loop(32, image)
    copies.start(q_ref, q_hbm)
    spread(q_ref, zq_ref, 1, copies, zq_hbm)
    rz = dot_core(f_ref, a_ref)
    pq = dot_core(a_ref, q_ref)
    pre_relax(
        q_ref, b_ref, e_ref, a_ref, (uxs_ref, uy_ref, uz_ref, d_ref, di_ref), lambda: copies.start(e_ref, e2_hbm)
    )
    restrict_fine(a_ref, m1_ref, 0)
    qw = dot_core(e_ref, q_ref, a_ref)
    lane = lane_id((8, 128))
    dots_ref[...] = jnp.where(lane == 0, rz, jnp.where(lane == 1, pq, jnp.where(lane == 2, qw, 0.0)))
    copies.finish()


def last_kernel(
    l1, ll, lr, f1, fl, fr, uxs_hbm, uy_hbm, uz_hbm, di_hbm, q_hbm, e_hbm, dots_ref,
    wo_hbm, line_ref,
    uxs_ref, uy_ref, uz_ref, di_ref, q_ref, e_ref, wo_ref, a_ref, b_ref, p_ref, c_ref, *rest,
):
    copies = Copies(rest[-1])
    load1(copies, (l1, ll, lr), (f1, fl, fr), rest)
    small, copies.open = copies.open, []
    for src, dst in ((e_hbm, e_ref), (uxs_hbm, uxs_ref), (uy_hbm, uy_ref), (uz_hbm, uz_ref), (di_hbm, di_ref),
                     (q_hbm, q_ref)):
        copies.start(src, dst)
    for copy in small:
        copy.wait()
    energy = coarse_solve(c_ref, *rest[:-1])
    line_ref[...] = dots_ref[...] + jnp.where(lane_id((8, 128)) == 2, energy, 0.0)
    copies.finish()
    add_coarse(e_ref, c_ref, a_ref, p_ref)
    post_relax(q_ref, a_ref, b_ref, (uxs_ref, uy_ref, uz_ref, di_ref))
    spread(a_ref, wo_ref, 0, copies, wo_hbm)
    copies.finish()


def load1(copies, weights, target, scratch):
    ux1, uy1, uz1, f1, t1 = scratch[0], scratch[1], scratch[2], scratch[3], scratch[8]
    for (core, left, right), field, dst, at in (
        (weights, 2, ux1, 1), (weights, 3, uy1, 0), (weights, 4, uz1, 0), (weights, 1, t1, 0), (target, 0, f1, 0),
    ):
        for src, low, n in ((left, 0, 24), (core, 24, 32), (right, 56, 24)):
            copies.start(src.at[field], dst.at[pl.ds(at, 8), pl.ds(low, n)])


def pair1(v_ref, x, both_x, upper_z):
    total = v_ref[x, pl.ds(1, 40, stride=2), :]
    if not upper_z:
        total = total + v_ref[x, pl.ds(0, 40, stride=2), :]
    if both_x:
        total = total + pair1(v_ref, x + 1, False, upper_z)
    return total


def coarse_solve(
    o_ref, ux1, uy1, uz1, f1, d1, di1, v1, v1b, t1, ux2, uy2, uz2, f2, di2, v2, v2b, p_ref
):
    ux1[0] = lanes(ux1[8], 1)

    valid = lane_id((40, 128)) % 4 < 2

    def fold(v):
        return jnp.where(valid, v, 0.0)

    for x in range(4):
        a = pair1(ux1, 2 * x + 2, False, False)
        ux2[x + 1] = fold(a + lanes(a, -2))
        uy2[x] = fold(lanes(pair1(uy1, 2 * x, True, False), -2))
        a = pair1(uz1, 2 * x, True, True)
        uz2[x] = fold(a + lanes(a, -2))
    ux2[0] = lanes(ux2[4], 1)
    for x in range(4):
        a = pair1(t1, 2 * x, True, False)
        d = diagonal(fold(a + lanes(a, -2)), ux2, uy2, uz2, x, 4)
        di2[x] = jnp.where(d > 0.0, OMEGA / d, 0.0)

    def setup(x):
        d = diagonal(t1[x], ux1, uy1, uz1, x, 2)
        di = jnp.where(d > 0.0, OMEGA / d, 0.0)
        d1[x] = d
        di1[x] = di
        v1[x + 1] = di * f1[x]

    loop(8, setup)

    def relax1(src, dst):
        ghosts(src, 8)

        def sweep(x):
            v, total = neighbours(src, ux1, uy1, uz1, x, 2, True)
            dst[x + 1] = KEEP * v + di1[x] * (f1[x] + total)

        loop(8, sweep)

    relax1(v1, v1b)
    ghosts(v1b, 8)

    dot = jnp.zeros((32, 128), F32)
    for x in range(8):
        v, total = neighbours(v1b, ux1, uy1, uz1, x, 2, True)
        f = f1[x]
        r = f - d1[x] * v + total
        t1[x] = r
        dot = dot + (v * (f + r))[24:56]

    for x in range(4):
        a = pair1(t1, 2 * x, True, False)
        f2[x] = fold(a + lanes(a, -2))
        v2[x + 1] = di2[x] * f2[x]
    src, dst = v2, v2b
    for _ in range(COARSE_SWEEPS - 1):
        ghosts(src, 4)
        for x in range(4):
            v, total = neighbours(src, ux2, uy2, uz2, x, 4, True)
            dst[x + 1] = KEEP * v + di2[x] * (f2[x] + total)
        src, dst = dst, src

    low = row_id((40, 128))
    own = (low >= 12) & (low < 28)
    dot2 = jnp.zeros((40, 128), F32)
    for x in range(4):
        dot2 = dot2 + jnp.where(own, src[x + 1] * f2[x], 0.0)
    energy = jnp.sum(dot) + jnp.sum(dot2)

    for x in range(4):
        w = src[x + 1]
        w = w + lanes(w, 2)
        p_ref[x, pl.ds(0, 40, stride=2), :] = w
        p_ref[x, pl.ds(1, 40, stride=2), :] = w
        wide = p_ref[x]
        v1b[2 * x + 1] = v1b[2 * x + 1] + wide
        v1b[2 * x + 2] = v1b[2 * x + 2] + wide
    relax1(v1b, v1)
    relax1(v1, v1b)
    for x in range(8):
        o_ref[x] = v1b[x + 1, 20:60]
    return energy


def output_kernel(odd_ref, seed_ref, zq_ref, w_ref, sol_ref, res_ref, dir_ref):
    label = pl.program_id(0)
    odd = odd_ref[0]
    sums = w_ref[0, 128:136, :] + w_ref[1, 128:136, :]
    rz, pq, qw = sums[0:1, 0:1], sums[0:1, 1:2], sums[0:1, 2:3]
    step = rz / pq
    more = (step * step * qw) / rz
    low = lane_id((32, 128)) < 64
    for x in range(4):
        pair = []
        for ref, at in ((zq_ref, x), (zq_ref, x + 4), (w_ref, x)):
            a, b = ref[odd, 32 * at : 32 * at + 32], ref[1 - odd, 32 * at : 32 * at + 32]
            pair.append((jnp.where(low, a, lanes(b, 64)), jnp.where(low, lanes(a, 64), b)))
        for k in range(2):
            z, q, w = pair[0][k], pair[1][k], pair[2][k]
            at = x + 4 * k
            f = jnp.where(seed_ref[at] == label, PENALTY, 0.0)
            sol_ref[0, at] = step * z
            res_ref[0, at] = f - step * q
            dir_ref[0, at] = more * z - step * w


def sds(*shape):
    return jax.ShapeDtypeStruct(shape, F32)


def call(kernel, out, args, smem=0, vmem=0, scratch=(), sems=0, cost=1000000, name=None):
    here, scalar = pl.BlockSpec(memory_space=pltpu.VMEM), pl.BlockSpec(memory_space=pltpu.SMEM)
    away = pl.BlockSpec(memory_space=pl.ANY)
    args = list(args)
    for k in range(smem, len(args) - vmem):
        if args[k].shape in (FINE, TALL):
            args[k] = pltpu.with_memory_space_constraint(args[k], pltpu.HBM)
    return pl.pallas_call(
        kernel,
        out_shape=[pltpu.HBM(shape, F32) if far else sds(*shape) for shape, far in out],
        in_specs=[scalar] * smem + [away] * (len(args) - smem - vmem) + [here] * vmem,
        out_specs=[pl.BlockSpec(memory_space=pltpu.HBM) if far else here for _, far in out],
        scratch_shapes=[pltpu.VMEM(s, F32) for s in scratch] + ([pltpu.SemaphoreType.DMA((sems,))] if sems else []),
        compiler_params=pltpu.CompilerParams(vmem_limit_bytes=VLIMIT),
        cost_estimate=pl.CostEstimate(flops=cost, bytes_accessed=cost, transcendentals=0),
        name=name,
    )(*args)


FINE = (32, 80, 128)
TALL = (33, 80, 128)
LEVEL1 = (8, 80, 128)
LEVEL2 = (4, 40, 128)
COARSE = (
    [(9, 80, 128)] + [LEVEL1] * 5 + [(10, 80, 128)] * 2 + [LEVEL1]
    + [(5, 40, 128)] + [LEVEL2] * 4 + [(6, 40, 128)] * 2 + [(4, 80, 128)]
)


def z_chain():
    def at(label, gz, half):
        return (2 * label + (half ^ (gz & 1))) * 8 + gz

    pairs = []
    for label in range(LABELS):
        for gz in range(8):
            pairs.append((at(label, gz, 0), at(label, gz, 1)))
            if gz < 7:
                pairs.append((at(label, gz, 1), at(label, gz + 1, 0)))
    return pairs


def swap(first, last):
    every = ("gx", "gy", "gz")
    up = z_chain()
    down = [(b, a) for a, b in up]
    return lax.ppermute(last, every, up), lax.ppermute(first, every, down)


def swap1(v):
    return swap(v[:, :, 0:24], v[:, :, 8:32])


def local(intensity, seed_labels):
    gx, gy, gz = lax.axis_index("gx"), lax.axis_index("gy"), lax.axis_index("gz")
    group = ("gx", "gy")
    odd = (gz & 1).reshape(1)
    half = (gy ^ gz) & 1
    label = ((4 * gx + gy) // 2).reshape(1)
    z_base = (128 * gz + 64 * half).reshape(1)

    sent = call(
        pack_kernel, [((16, 8, 32, 128), False)], (odd, intensity, seed_labels), smem=1, vmem=2, name="pack"
    )[0]
    got = lax.all_to_all(sent, group, 0, 0, tiled=True)
    core, first, last = call(
        assemble_kernel,
        [((64, 64, 128), False), ((64, 8, 128), False), ((64, 8, 128), False)],
        (got,),
        vmem=1,
        name="turn",
    )
    left, right = swap(first, last)
    uxs, uy, uz, d, di, f, e, l1 = call(
        first_kernel,
        [(TALL, True)] + [(FINE, True)] * 6 + [((5, 8, 32, 128), False)],
        (z_base, label, core, left, right),
        smem=2,
        scratch=[TALL] + [FINE] * 8,
        sems=13,
        name="first",
    )
    ll, lr = swap1(l1)
    zq, q, e2, m1, dots = call(
        middle_kernel,
        [((16, 256, 128), True), (FINE, True), (FINE, True), ((1, 8, 32, 128), False), ((8, 128), False)],
        (l1, ll, lr, l1, ll, lr, uxs, uy, uz, d, di, f, e),
        scratch=[TALL] + [FINE] * 6 + [(16, 256, 128)] + [FINE] * 3 + [(8, 80, 128), (8, 40, 128)] + COARSE,
        sems=32,
        name="middle",
    )
    ml, mr = swap1(m1)
    zq, ml, mr = lax.optimization_barrier((zq, ml, mr))
    zqr = lax.all_to_all(zq, group, 0, 0, tiled=True)
    wo, line = call(
        last_kernel,
        [((16, 136, 128), True), ((8, 128), False)],
        (l1, ll, lr, m1, ml, mr, uxs, uy, uz, di, q, e2, dots),
        vmem=1,
        scratch=[TALL] + [FINE] * 5 + [(16, 128, 128)] + [FINE] * 2 + [(8, 80, 128), (8, 40, 128)] + COARSE,
        sems=25,
        name="last",
    )
    sums = lax.psum(line, "gz")
    wo, zqr = lax.optimization_barrier((wo, zqr))
    wo = lax.dynamic_update_slice(wo, jnp.broadcast_to(sums, (16, 8, 128)), (0, 128, 0))
    wr_ = lax.all_to_all(wo, group, 0, 0, tiled=True)

    smem = pl.BlockSpec(memory_space=pltpu.SMEM)
    return tuple(
        pl.pallas_call(
            output_kernel,
            grid=(LABELS,),
            out_shape=[sds(8, 8, 32, 128)] * 3,
            in_specs=[
                smem,
                pl.BlockSpec((8, 32, 128), lambda i: (0, 0, 0)),
                pl.BlockSpec((2, 256, 128), lambda i: (i, 0, 0)),
                pl.BlockSpec((2, 136, 128), lambda i: (i, 0, 0)),
            ],
            out_specs=[pl.BlockSpec((1, 8, 32, 128), lambda i: (i, 0, 0, 0))] * 3,
            compiler_params=pltpu.CompilerParams(vmem_limit_bytes=VLIMIT),
            name="output",
        )(odd, seed_labels, zqr, wr_)
    )


def solution(mesh):
    placed = (P("gx", "gy", "gz"), P("gx", "gy", "gz"))
    return jax.shard_map(
        local,
        mesh=mesh,
        in_specs=placed,
        out_specs=(P(None, "gx", "gy", "gz"), P(None, "gx", "gy", "gz"), P(None, "gx", "gy", "gz")),
        check_vma=False,
    )
```

```python
import functools

import jax
import jax.numpy as jnp
from jax import lax
from jax.experimental import pallas as pl
from jax.experimental.pallas import tpu as pltpu
from jax.sharding import PartitionSpec as P


LABELS = 8
BETA = 0.5
WFLOOR = 0.01
REACT = 0.01
PENALTY = 4.0
OMEGA = 0.8
KEEP = 1.0 - OMEGA
COARSE_SWEEPS = 6
VLIMIT = 44 * 1024 * 1024
F32 = jnp.float32


def lanes(v, shift):
    return pltpu.roll(v, shift % 128, 1)


def rows(v, shift):
    return pltpu.roll(v, shift % v.shape[0], 0)


def loop(n, body, group=16, acc=None):
    def step(i, c):
        sums = {}
        for k in range(min(group, n)):
            for slot, v in enumerate(body(group * i + k) or ()):
                if v is not None and acc is not None:
                    sums[slot] = sums[slot] + v if slot in sums else v
        for slot, v in sums.items():
            acc[slot] += v
        return c

    if n <= group:
        step(0, 0)
    else:
        lax.fori_loop(0, n // group, step, 0)


class Copies:
    def __init__(self, sems):
        self.sems, self.used, self.open = sems, 0, []

    def start(self, src, dst):
        copy = pltpu.make_async_copy(src, dst, self.sems.at[self.used])
        copy.start()
        self.used += 1
        self.open.append(copy)
        return copy

    def finish(self):
        for copy in self.open:
            copy.wait()
        self.open = []


def lane_id(shape):
    return lax.broadcasted_iota(jnp.int32, shape, 1)


def row_id(shape):
    return lax.broadcasted_iota(jnp.int32, shape, 0)


def neighbours(v_ref, uxs_ref, uy_ref, uz_ref, x, stride, ghost):
    if ghost:
        below, v, above = v_ref[x], v_ref[x + 1], v_ref[x + 2]
    else:
        last = v_ref.shape[0] - 1
        below, v, above = v_ref[jnp.maximum(x - 1, 0)], v_ref[x], v_ref[jnp.minimum(x + 1, last)]
    uy, uz = uy_ref[x], uz_ref[x]
    total = uxs_ref[x + 1] * above + uxs_ref[x] * below
    total = total + uy * lanes(v, -stride) + lanes(uy * v, stride)
    total = total + uz * rows(v, -1) + rows(uz * v, 1)
    return v, total


def diagonal(source, uxs_ref, uy_ref, uz_ref, x, stride):
    uy, uz = uy_ref[x], uz_ref[x]
    return source + uxs_ref[x + 1] + uxs_ref[x] + uy + lanes(uy, stride) + uz + rows(uz, 1)


def ghosts(v_ref, n):
    v_ref[0] = lanes(v_ref[n], 1)
    v_ref[n + 1] = lanes(v_ref[1], -1)


def pack_kernel(odd_ref, i_hbm, s_hbm, o_ref, i_ref, s_ref, sems):
    copies = Copies(sems)
    copies.start(i_hbm, i_ref)
    copies.start(s_hbm, s_ref)
    copies.finish()
    odd = odd_ref[0]
    low = lane_id((32, 128)) < 64
    for field, v_ref in enumerate((i_ref, s_ref)):
        parts = ([], [])
        for x in range(4):
            a, b = v_ref[x].astype(F32), v_ref[x + 4].astype(F32)
            parts[0].append(jnp.where(low, a, lanes(b, 64)))
            parts[1].append(jnp.where(low, lanes(a, 64), b))
        for label in range(LABELS):
            for half in range(2):
                slot = 2 * label + jnp.bitwise_xor(odd, half)
                for k in range(4):
                    o_ref[slot, 4 * field + k] = parts[half][k]


def assemble_kernel(r_ref, core_ref, first_ref, last_ref):
    for gx in range(4):
        for k in range(8):
            turned = r_ref[4 * gx : 4 * gx + 4, k].reshape(128, 128).T
            for part in range(2):
                x = 32 * (k // 4) + 8 * gx + k % 4 + 4 * part
                core_ref[x] = turned[64 * part : 64 * part + 64]
                first_ref[x] = turned[64 * part : 64 * part + 8]
                last_ref[x] = turned[64 * part + 56 : 64 * part + 64]


def spread(v_ref, o_ref, field, copies, out_ref):
    for gx in range(4):
        for k in range(4):
            a, b = v_ref[8 * gx + k, 8:72], v_ref[8 * gx + k + 4, 8:72]
            turned = jnp.concatenate([a, b], axis=0).T.reshape(4, 32, 128)
            o_ref[4 * gx : 4 * gx + 4, 32 * (4 * field + k) : 32 * (4 * field + k + 1)] = turned
        part = (pl.ds(4 * gx, 4), pl.ds(128 * field, 128))
        copies.start(o_ref.at[part], out_ref.at[part])


def plane_pair(v_ref, x, both_x, upper_z):
    total = v_ref[x, pl.ds(9, 32, stride=2), :]
    if not upper_z:
        total = total + v_ref[x, pl.ds(8, 32, stride=2), :]
    if both_x:
        total = total + plane_pair(v_ref, x + 1, False, upper_z)
    return total


def pack_pair(a, b):
    even = lane_id(a.shape) % 2 == 0
    return jnp.where(even, a + lanes(a, -1), b + lanes(b, 1))


def restrict_fine(v_ref, o_ref, slot):
    def body(x):
        a = plane_pair(v_ref, 2 * x, True, False)
        b = plane_pair(v_ref, 2 * x + 16, True, False)
        o_ref[slot, x] = pack_pair(a, b)

    loop(8, body)


def edge_weight(contrast):
    return jnp.exp(-BETA * contrast * contrast) + WFLOOR


def pre_relax(f_ref, g_ref, e_ref, t_ref, level, then, acc=None):
    uxs_ref, uy_ref, uz_ref, d_ref, di_ref = level

    def sweep(x):
        v, total = neighbours(g_ref, uxs_ref, uy_ref, uz_ref, x, 1, False)
        e_ref[x] = KEEP * v + di_ref[x] * (f_ref[x] + total)

    loop(32, sweep)
    then()

    def rest(x):
        v, total = neighbours(e_ref, uxs_ref, uy_ref, uz_ref, x, 1, False)
        f = f_ref[x]
        t = f - d_ref[x] * v + total
        t_ref[x] = t
        return (None, None, (v * (f + t))[8:72])

    loop(32, rest, acc=acc)


def first_kernel(
    zb_ref, lab_ref, core_hbm, left_hbm, right_hbm,
    uxs_hbm, uy_hbm, uz_hbm, d_hbm, di_hbm, f_hbm, e_hbm, l1_ref,
    uxs_ref, uy_ref, uz_ref, d_ref, di_ref, f_ref, e_ref, v_ref, s_ref, sems,
):
    copies = Copies(sems)
    for base, dst in ((0, v_ref), (32, s_ref)):
        for src, at, n in ((left_hbm, 0, 8), (core_hbm, 8, 64), (right_hbm, 72, 8)):
            copies.start(src.at[pl.ds(base, 32)], dst.at[:, pl.ds(at, n)])
    arrived, copies.open = copies.open, []
    for copy in arrived[:3]:
        copy.wait()
    lane = lane_id((80, 128))
    place = row_id((80, 128)) + (zb_ref[0] - 8)
    cut = (place == -1) | (place == 1023)
    uxs_ref[0] = jnp.zeros((80, 128), F32)

    def body(x):
        v = v_ref[x]
        above = v_ref[jnp.minimum(x + 1, 31)]
        uxs_ref[x + 1] = jnp.where(x == 31, 0.0, edge_weight(above - v))
        uy_ref[x] = jnp.where(lane == 127, 0.0, edge_weight(lanes(v, -1) - v))
        uz_ref[x] = jnp.where(cut, 0.0, edge_weight(rows(v, -1) - v))

    loop(32, body, 4)
    even = lane_id((32, 128)) % 2 == 0

    def coarse(x):
        l1_ref[2, x] = pack_pair(
            plane_pair(uxs_ref, 2 * x + 2, False, False), plane_pair(uxs_ref, 2 * x + 18, False, False)
        )
        a, b = plane_pair(uy_ref, 2 * x, True, False), plane_pair(uy_ref, 2 * x + 16, True, False)
        l1_ref[3, x] = jnp.where(even, lanes(a, -1), b)
        l1_ref[4, x] = pack_pair(
            plane_pair(uz_ref, 2 * x, True, True), plane_pair(uz_ref, 2 * x + 16, True, True)
        )

    loop(8, coarse)
    copies.start(uxs_ref, uxs_hbm)
    copies.start(uy_ref, uy_hbm)
    copies.start(uz_ref, uz_hbm)
    for copy in arrived[3:]:
        copy.wait()
    label = lab_ref[0].astype(F32)

    def setup(x):
        seed = s_ref[x]
        f = jnp.where(seed == label, PENALTY, 0.0)
        source = jnp.where(seed >= 0.0, REACT + PENALTY, REACT)
        d = diagonal(source, uxs_ref, uy_ref, uz_ref, x, 1)
        di = OMEGA / d
        s_ref[x] = source
        f_ref[x] = f
        d_ref[x] = d
        di_ref[x] = di
        v_ref[x] = di * f

    loop(32, setup)
    copies.start(d_ref, d_hbm)
    copies.start(di_ref, di_hbm)
    copies.start(f_ref, f_hbm)
    restrict_fine(s_ref, l1_ref, 1)
    pre_relax(f_ref, v_ref, e_ref, s_ref, (uxs_ref, uy_ref, uz_ref, d_ref, di_ref), lambda: copies.start(e_ref, e_hbm))
    restrict_fine(s_ref, l1_ref, 0)
    copies.finish()


def add_coarse(e_ref, c_ref, o_ref, p_ref):
    even = lane_id((40, 128)) % 2 == 0

    def body(x):
        v = c_ref[x]
        for part in range(2):
            if part == 0:
                w = jnp.where(even, v, 0.0)
                w = w + lanes(w, 1)
            else:
                w = jnp.where(even, 0.0, v)
                w = w + lanes(w, -1)
            at = 2 * x + 16 * part
            slot = x % 4 + 4 * part
            p_ref[slot, pl.ds(0, 40, stride=2), :] = w
            p_ref[slot, pl.ds(1, 40, stride=2), :] = w
            wide = p_ref[slot]
            o_ref[at] = e_ref[at] + wide
            o_ref[at + 1] = e_ref[at + 1] + wide

    loop(8, body)


def post_relax(f_ref, a_ref, b_ref, level):
    uxs_ref, uy_ref, uz_ref, di_ref = level
    for src, dst in ((a_ref, b_ref), (b_ref, a_ref)):

        def sweep(x):
            v, total = neighbours(src, uxs_ref, uy_ref, uz_ref, x, 1, False)
            dst[x] = KEEP * v + di_ref[x] * (f_ref[x] + total)

        loop(32, sweep)


def middle_kernel(
    l1, ll, lr, f1, fl, fr, uxs_hbm, uy_hbm, uz_hbm, d_hbm, di_hbm, f_hbm, e_hbm,
    zq_hbm, q_hbm, e2_hbm, m1_ref, dots_ref,
    uxs_ref, uy_ref, uz_ref, d_ref, di_ref, f_ref, e_ref, zq_ref, q_ref, a_ref, b_ref, dots_acc, p_ref, c_ref, *rest,
):
    copies = Copies(rest[-1])
    load1(copies, (l1, ll, lr), (f1, fl, fr), rest)
    small, copies.open = copies.open, []
    for src, dst in ((e_hbm, e_ref), (uxs_hbm, uxs_ref), (uy_hbm, uy_ref), (uz_hbm, uz_ref), (di_hbm, di_ref),
                     (f_hbm, f_ref), (d_hbm, d_ref)):
        copies.start(src, dst)
    for copy in small:
        copy.wait()
    coarse_solve(c_ref, *rest[:-1])
    copies.finish()
    add_coarse(e_ref, c_ref, a_ref, p_ref)
    post_relax(f_ref, a_ref, b_ref, (uxs_ref, uy_ref, uz_ref, di_ref))
    spread(a_ref, zq_ref, 0, copies, zq_hbm)

    def image(x):
        v, total = neighbours(a_ref, uxs_ref, uy_ref, uz_ref, x, 1, False)
        q = d_ref[x] * v - total
        q_ref[x] = q
        b_ref[x] = di_ref[x] * q
        return (f_ref[x] * v)[8:72], (v * q)[8:72]

    dots_acc[...] = jnp.zeros_like(dots_acc)
    loop(32, image, acc=dots_acc)
    copies.start(q_ref, q_hbm)
    spread(q_ref, zq_ref, 1, copies, zq_hbm)
    pre_relax(
        q_ref, b_ref, e_ref, a_ref, (uxs_ref, uy_ref, uz_ref, d_ref, di_ref),
        lambda: copies.start(e_ref, e2_hbm), dots_acc,
    )
    restrict_fine(a_ref, m1_ref, 0)
    rz, pq, qw = jnp.sum(dots_acc[0]), jnp.sum(dots_acc[1]), jnp.sum(dots_acc[2])
    lane = lane_id((8, 128))
    dots_ref[...] = jnp.where(lane == 0, rz, jnp.where(lane == 1, pq, jnp.where(lane == 2, qw, 0.0)))
    copies.finish()


def last_kernel(
    lab_ref, l1, ll, lr, f1, fl, fr, uxs_hbm, uy_hbm, uz_hbm, di_hbm, q_hbm, e_hbm, dots_ref,
    wo_hbm, line_ref,
    uxs_ref, uy_ref, uz_ref, di_ref, q_ref, e_ref, wo_ref, a_ref, b_ref, p_ref, c_ref, *rest,
):
    copies = Copies(rest[-1])
    load1(copies, (l1, ll, lr), (f1, fl, fr), rest)
    small, copies.open = copies.open, []
    for src, dst in ((e_hbm, e_ref), (uxs_hbm, uxs_ref), (uy_hbm, uy_ref), (uz_hbm, uz_ref), (di_hbm, di_ref),
                     (q_hbm, q_ref)):
        copies.start(src, dst)
    for copy in small:
        copy.wait()
    energy = coarse_solve(c_ref, *rest[:-1])
    line = dots_ref[...] + jnp.where(lane_id((8, 128)) == 2, energy, 0.0)
    line_ref[...] = jnp.where(row_id((8, 128)) == lab_ref[0], line, 0.0)
    copies.finish()
    add_coarse(e_ref, c_ref, a_ref, p_ref)
    post_relax(q_ref, a_ref, b_ref, (uxs_ref, uy_ref, uz_ref, di_ref))
    spread(a_ref, wo_ref, 0, copies, wo_hbm)
    copies.finish()


def load1(copies, weights, target, scratch):
    ux1, uy1, uz1, f1, t1 = scratch[0], scratch[1], scratch[2], scratch[3], scratch[8]
    for (core, left, right), field, dst, at in (
        (weights, 2, ux1, 1), (weights, 3, uy1, 0), (weights, 4, uz1, 0), (weights, 1, t1, 0), (target, 0, f1, 0),
    ):
        for src, low, n in ((left, 0, 24), (core, 24, 32), (right, 56, 24)):
            copies.start(src.at[field], dst.at[pl.ds(at, 8), pl.ds(low, n)])


def pair1(v_ref, x, both_x, upper_z):
    total = v_ref[x, pl.ds(1, 40, stride=2), :]
    if not upper_z:
        total = total + v_ref[x, pl.ds(0, 40, stride=2), :]
    if both_x:
        total = total + pair1(v_ref, x + 1, False, upper_z)
    return total


def coarse_solve(
    o_ref, ux1, uy1, uz1, f1, d1, di1, v1, v1b, t1, ux2, uy2, uz2, f2, di2, v2, v2b, p_ref
):
    ux1[0] = lanes(ux1[8], 1)

    valid = lane_id((40, 128)) % 4 < 2

    def fold(v):
        return jnp.where(valid, v, 0.0)

    for x in range(4):
        a = pair1(ux1, 2 * x + 2, False, False)
        ux2[x + 1] = fold(a + lanes(a, -2))
        uy2[x] = fold(lanes(pair1(uy1, 2 * x, True, False), -2))
        a = pair1(uz1, 2 * x, True, True)
        uz2[x] = fold(a + lanes(a, -2))
    ux2[0] = lanes(ux2[4], 1)
    for x in range(4):
        a = pair1(t1, 2 * x, True, False)
        d = diagonal(fold(a + lanes(a, -2)), ux2, uy2, uz2, x, 4)
        di2[x] = jnp.where(d > 0.0, OMEGA / d, 0.0)

    def setup(x):
        d = diagonal(t1[x], ux1, uy1, uz1, x, 2)
        di = jnp.where(d > 0.0, OMEGA / d, 0.0)
        d1[x] = d
        di1[x] = di
        v1[x + 1] = di * f1[x]

    loop(8, setup)

    def relax1(src, dst):
        ghosts(src, 8)

        def sweep(x):
            v, total = neighbours(src, ux1, uy1, uz1, x, 2, True)
            dst[x + 1] = KEEP * v + di1[x] * (f1[x] + total)

        loop(8, sweep)

    relax1(v1, v1b)
    ghosts(v1b, 8)

    dot = jnp.zeros((32, 128), F32)
    for x in range(8):
        v, total = neighbours(v1b, ux1, uy1, uz1, x, 2, True)
        f = f1[x]
        r = f - d1[x] * v + total
        t1[x] = r
        dot = dot + (v * (f + r))[24:56]

    for x in range(4):
        a = pair1(t1, 2 * x, True, False)
        f2[x] = fold(a + lanes(a, -2))
        v2[x + 1] = di2[x] * f2[x]
    src, dst = v2, v2b
    for _ in range(COARSE_SWEEPS - 1):
        ghosts(src, 4)
        for x in range(4):
            v, total = neighbours(src, ux2, uy2, uz2, x, 4, True)
            dst[x + 1] = KEEP * v + di2[x] * (f2[x] + total)
        src, dst = dst, src

    low = row_id((40, 128))
    own = (low >= 12) & (low < 28)
    dot2 = jnp.zeros((40, 128), F32)
    for x in range(4):
        dot2 = dot2 + jnp.where(own, src[x + 1] * f2[x], 0.0)
    energy = jnp.sum(dot) + jnp.sum(dot2)

    for x in range(4):
        w = src[x + 1]
        w = w + lanes(w, 2)
        p_ref[x, pl.ds(0, 40, stride=2), :] = w
        p_ref[x, pl.ds(1, 40, stride=2), :] = w
        wide = p_ref[x]
        v1b[2 * x + 1] = v1b[2 * x + 1] + wide
        v1b[2 * x + 2] = v1b[2 * x + 2] + wide
    relax1(v1b, v1)
    relax1(v1, v1b)
    for x in range(8):
        o_ref[x] = v1b[x + 1, 20:60]
    return energy


def output_kernel(odd_ref, seed_ref, sums_ref, zq_ref, w_ref, sol_ref, res_ref, dir_ref):
    odd = odd_ref[0]
    everyone = jnp.sum(sums_ref[...], axis=0)
    low = lane_id((32, 128)) < 64
    for j in range(2):
        label = 2 * pl.program_id(0) + j
        sums = jnp.sum(jnp.where(row_id((8, 128)) == label, everyone, 0.0), axis=0, keepdims=True)
        rz, pq, qw = sums[:, 0:1], sums[:, 1:2], sums[:, 2:3]
        step = rz / pq
        more = (step * step * qw) / rz
        for x in range(4):
            pair = []
            for ref, at in ((zq_ref, x), (zq_ref, x + 4), (w_ref, x)):
                a, b = ref[2 * j + odd, 32 * at : 32 * at + 32], ref[2 * j + 1 - odd, 32 * at : 32 * at + 32]
                pair.append((jnp.where(low, a, lanes(b, 64)), jnp.where(low, lanes(a, 64), b)))
            for k in range(2):
                z, q, w = pair[0][k], pair[1][k], pair[2][k]
                at = x + 4 * k
                f = jnp.where(seed_ref[at] == label, PENALTY, 0.0)
                sol_ref[j, at] = step * z
                res_ref[j, at] = f - step * q
                dir_ref[j, at] = more * z - step * w


def sds(*shape):
    return jax.ShapeDtypeStruct(shape, F32)


def call(kernel, out, args, smem=0, vmem=0, scratch=(), sems=0, cost=1000000, name=None):
    here, scalar = pl.BlockSpec(memory_space=pltpu.VMEM), pl.BlockSpec(memory_space=pltpu.SMEM)
    away = pl.BlockSpec(memory_space=pl.ANY)
    args = list(args)
    for k in range(smem, len(args) - vmem):
        if args[k].shape in (FINE, TALL, (8, 32, 128)):
            args[k] = pltpu.with_memory_space_constraint(args[k], pltpu.HBM)
    return pl.pallas_call(
        kernel,
        out_shape=[pltpu.HBM(shape, F32) if far else sds(*shape) for shape, far in out],
        in_specs=[scalar] * smem + [away] * (len(args) - smem - vmem) + [here] * vmem,
        out_specs=[pl.BlockSpec(memory_space=pltpu.HBM) if far else here for _, far in out],
        scratch_shapes=[pltpu.VMEM(s, F32) if isinstance(s, tuple) else s for s in scratch] + ([pltpu.SemaphoreType.DMA((sems,))] if sems else []),
        compiler_params=pltpu.CompilerParams(vmem_limit_bytes=VLIMIT),
        cost_estimate=pl.CostEstimate(flops=cost, bytes_accessed=cost, transcendentals=0),
        name=name,
    )(*args)


FINE = (32, 80, 128)
TALL = (33, 80, 128)
LEVEL1 = (8, 80, 128)
LEVEL2 = (4, 40, 128)
COARSE = (
    [(9, 80, 128)] + [LEVEL1] * 5 + [(10, 80, 128)] * 2 + [LEVEL1]
    + [(5, 40, 128)] + [LEVEL2] * 4 + [(6, 40, 128)] * 2 + [(4, 80, 128)]
)


def z_chain():
    def at(label, gz, half):
        return (2 * label + (half ^ (gz & 1))) * 8 + gz

    pairs = []
    for label in range(LABELS):
        for gz in range(8):
            pairs.append((at(label, gz, 0), at(label, gz, 1)))
            if gz < 7:
                pairs.append((at(label, gz, 1), at(label, gz + 1, 0)))
    return pairs


def swap(first, last):
    every = ("gx", "gy", "gz")
    up = z_chain()
    down = [(b, a) for a, b in up]
    return lax.ppermute(last, every, up), lax.ppermute(first, every, down)


def swap1(v):
    return swap(v[:, :, 0:24], v[:, :, 8:32])


def local(intensity, seed_labels):
    gx, gy, gz = lax.axis_index("gx"), lax.axis_index("gy"), lax.axis_index("gz")
    group = ("gx", "gy")
    odd = (gz & 1).reshape(1)
    half = (gy ^ gz) & 1
    label = ((4 * gx + gy) // 2).reshape(1)
    z_base = (128 * gz + 64 * half).reshape(1)

    sent = call(
        pack_kernel, [((16, 8, 32, 128), False)], (odd, intensity, seed_labels), smem=1,
        scratch=[(8, 32, 128), pltpu.VMEM((8, 32, 128), jnp.int32)], sems=2, name="pack",
    )[0]
    got = lax.all_to_all(sent, group, 0, 0, tiled=True)
    core, first, last = call(
        assemble_kernel,
        [((64, 64, 128), False), ((64, 8, 128), False), ((64, 8, 128), False)],
        (got,),
        vmem=1,
        name="turn",
    )
    left, right = swap(first, last)
    uxs, uy, uz, d, di, f, e, l1 = call(
        first_kernel,
        [(TALL, True)] + [(FINE, True)] * 6 + [((5, 8, 32, 128), False)],
        (z_base, label, core, left, right),
        smem=2,
        scratch=[TALL] + [FINE] * 8,
        sems=13,
        name="first",
    )
    ll, lr = swap1(l1)
    zq, q, e2, m1, dots = call(
        middle_kernel,
        [((16, 256, 128), True), (FINE, True), (FINE, True), ((1, 8, 32, 128), False), ((8, 128), False)],
        (l1, ll, lr, l1, ll, lr, uxs, uy, uz, d, di, f, e),
        scratch=[TALL] + [FINE] * 6 + [(16, 256, 128)] + [FINE] * 3 + [(3, 64, 128), (8, 80, 128), (8, 40, 128)] + COARSE,
        sems=32,
        name="middle",
    )
    ml, mr = swap1(m1)
    zq, ml, mr = lax.optimization_barrier((zq, ml, mr))
    zqr = lax.all_to_all(zq, group, 0, 0, tiled=True)
    wo, line = call(
        last_kernel,
        [((16, 136, 128), True), ((8, 128), False)],
        (label, l1, ll, lr, m1, ml, mr, uxs, uy, uz, di, q, e2, dots),
        smem=1,
        vmem=1,
        scratch=[TALL] + [FINE] * 5 + [(16, 128, 128)] + [FINE] * 2 + [(8, 80, 128), (8, 40, 128)] + COARSE,
        sems=25,
        name="last",
    )
    sums = lax.psum(line, "gz")
    wo, zqr = lax.optimization_barrier((wo, zqr))
    wo = lax.dynamic_update_slice(wo, jnp.broadcast_to(sums, (16, 8, 128)), (0, 128, 0))
    wr_ = lax.all_to_all(wo, group, 0, 0, tiled=True)

    return tuple(
        pl.pallas_call(
            output_kernel,
            grid=(LABELS // 2,),
            out_shape=[sds(8, 8, 32, 128)] * 3,
            in_specs=[
                pl.BlockSpec(memory_space=pltpu.SMEM),
                pl.BlockSpec((8, 32, 128), lambda i: (0, 0, 0)),
                pl.BlockSpec((16, 8, 128), lambda i: (0, 16, 0)),
                pl.BlockSpec((4, 256, 128), lambda i: (i, 0, 0)),
                pl.BlockSpec((4, 136, 128), lambda i: (i, 0, 0)),
            ],
            out_specs=[pl.BlockSpec((2, 8, 32, 128), lambda i: (i, 0, 0, 0))] * 3,
            compiler_params=pltpu.CompilerParams(vmem_limit_bytes=VLIMIT),
            name="output",
        )(odd, seed_labels, wr_, zqr, wr_)
    )


def solution(mesh):
    placed = (P("gx", "gy", "gz"), P("gx", "gy", "gz"))
    return jax.shard_map(
        local,
        mesh=mesh,
        in_specs=placed,
        out_specs=(P(None, "gx", "gy", "gz"), P(None, "gx", "gy", "gz"), P(None, "gx", "gy", "gz")),
        check_vma=False,
    )
```

```python
import functools

import jax
import jax.numpy as jnp
from jax import lax
from jax.experimental import pallas as pl
from jax.experimental.pallas import tpu as pltpu
from jax.sharding import PartitionSpec as P


LABELS = 8
BETA = 0.5
WFLOOR = 0.01
REACT = 0.01
PENALTY = 4.0
OMEGA = 0.8
KEEP = 1.0 - OMEGA
COARSE_SWEEPS = 6
VLIMIT = 44 * 1024 * 1024
F32 = jnp.float32


def lanes(v, shift):
    return pltpu.roll(v, shift % 128, 1)


def rows(v, shift):
    return pltpu.roll(v, shift % v.shape[0], 0)


def loop(n, body, group=16, acc=None):
    def step(i, c):
        sums = {}
        for k in range(min(group, n)):
            for slot, v in enumerate(body(group * i + k) or ()):
                if v is not None and acc is not None:
                    sums[slot] = sums[slot] + v if slot in sums else v
        for slot, v in sums.items():
            acc[slot] += v
        return c

    if n <= group:
        step(0, 0)
    else:
        lax.fori_loop(0, n // group, step, 0)


class Copies:
    def __init__(self, sems):
        self.sems, self.used, self.open = sems, 0, []

    def start(self, src, dst):
        copy = pltpu.make_async_copy(src, dst, self.sems.at[self.used])
        copy.start()
        self.used += 1
        self.open.append(copy)
        return copy

    def finish(self):
        for copy in self.open:
            copy.wait()
        self.open = []


def lane_id(shape):
    return lax.broadcasted_iota(jnp.int32, shape, 1)


def row_id(shape):
    return lax.broadcasted_iota(jnp.int32, shape, 0)


def neighbours(v_ref, uxs_ref, uy_ref, uz_ref, x, stride, ghost):
    if ghost:
        below, v, above = v_ref[x], v_ref[x + 1], v_ref[x + 2]
    else:
        last = v_ref.shape[0] - 1
        below, v, above = v_ref[jnp.maximum(x - 1, 0)], v_ref[x], v_ref[jnp.minimum(x + 1, last)]
    uy, uz = uy_ref[x], uz_ref[x]
    total = uxs_ref[x + 1] * above + uxs_ref[x] * below
    total = total + uy * lanes(v, -stride) + lanes(uy * v, stride)
    total = total + uz * rows(v, -1) + rows(uz * v, 1)
    return v, total


def diagonal(source, uxs_ref, uy_ref, uz_ref, x, stride):
    uy, uz = uy_ref[x], uz_ref[x]
    return source + uxs_ref[x + 1] + uxs_ref[x] + uy + lanes(uy, stride) + uz + rows(uz, 1)


def ghosts(v_ref, n):
    v_ref[0] = lanes(v_ref[n], 1)
    v_ref[n + 1] = lanes(v_ref[1], -1)


def pack_kernel(odd_ref, i_hbm, s_hbm, o_ref, i_ref, s_ref, sems):
    copies = Copies(sems)
    copies.start(i_hbm, i_ref)
    copies.start(s_hbm, s_ref)
    copies.finish()
    odd = odd_ref[0]
    low = lane_id((32, 128)) < 64
    for field, v_ref in enumerate((i_ref, s_ref)):
        parts = ([], [])
        for x in range(4):
            a, b = v_ref[x].astype(F32), v_ref[x + 4].astype(F32)
            parts[0].append(jnp.where(low, a, lanes(b, 64)))
            parts[1].append(jnp.where(low, lanes(a, 64), b))
        for label in range(LABELS):
            for half in range(2):
                slot = 2 * label + jnp.bitwise_xor(odd, half)
                for k in range(4):
                    o_ref[slot, 4 * field + k] = parts[half][k]


def assemble_kernel(r_ref, core_ref, first_ref, last_ref):
    for gx in range(4):
        for k in range(8):
            turned = r_ref[4 * gx : 4 * gx + 4, k].reshape(128, 128).T
            for part in range(2):
                x = 32 * (k // 4) + 8 * gx + k % 4 + 4 * part
                core_ref[x] = turned[64 * part : 64 * part + 64]
                first_ref[x] = turned[64 * part : 64 * part + 8]
                last_ref[x] = turned[64 * part + 56 : 64 * part + 64]


def spread(v_ref, o_ref, field, copies, out_ref):
    for gx in range(4):
        for k in range(4):
            a, b = v_ref[8 * gx + k, 8:72], v_ref[8 * gx + k + 4, 8:72]
            turned = jnp.concatenate([a, b], axis=0).T.reshape(4, 32, 128)
            o_ref[4 * gx : 4 * gx + 4, 32 * (4 * field + k) : 32 * (4 * field + k + 1)] = turned
        part = (pl.ds(4 * gx, 4), pl.ds(128 * field, 128))
        copies.start(o_ref.at[part], out_ref.at[part])


def plane_pair(v_ref, x, both_x, upper_z):
    total = v_ref[x, pl.ds(9, 32, stride=2), :]
    if not upper_z:
        total = total + v_ref[x, pl.ds(8, 32, stride=2), :]
    if both_x:
        total = total + plane_pair(v_ref, x + 1, False, upper_z)
    return total


def pack_pair(a, b):
    even = lane_id(a.shape) % 2 == 0
    return jnp.where(even, a + lanes(a, -1), b + lanes(b, 1))


def restrict_fine(v_ref, o_ref, slot):
    def body(x):
        a = plane_pair(v_ref, 2 * x, True, False)
        b = plane_pair(v_ref, 2 * x + 16, True, False)
        o_ref[slot, x] = pack_pair(a, b)

    loop(8, body)


def edge_weight(contrast):
    return jnp.exp(-BETA * contrast * contrast) + WFLOOR


def pre_relax(f_ref, g_ref, e_ref, t_ref, level, then, acc=None):
    uxs_ref, uy_ref, uz_ref, d_ref, di_ref = level

    def sweep(x):
        v, total = neighbours(g_ref, uxs_ref, uy_ref, uz_ref, x, 1, False)
        e_ref[x] = KEEP * v + di_ref[x] * (f_ref[x] + total)

    loop(32, sweep)
    then()

    def rest(x):
        v, total = neighbours(e_ref, uxs_ref, uy_ref, uz_ref, x, 1, False)
        f = f_ref[x]
        t = f - d_ref[x] * v + total
        t_ref[x] = t
        return (None, None, (v * (f + t))[8:72])

    loop(32, rest, acc=acc)


def first_kernel(
    zb_ref, lab_ref, core_hbm, left_hbm, right_hbm,
    uxs_hbm, uy_hbm, uz_hbm, d_hbm, di_hbm, f_hbm, e_hbm, l1_ref,
    uxs_ref, uy_ref, uz_ref, d_ref, di_ref, f_ref, e_ref, v_ref, s_ref, sems,
):
    copies = Copies(sems)
    for base, dst in ((0, v_ref), (32, s_ref)):
        for src, at, n in ((left_hbm, 0, 8), (core_hbm, 8, 64), (right_hbm, 72, 8)):
            copies.start(src.at[pl.ds(base, 32)], dst.at[:, pl.ds(at, n)])
    arrived, copies.open = copies.open, []
    for copy in arrived[:3]:
        copy.wait()
    lane = lane_id((80, 128))
    place = row_id((80, 128)) + (zb_ref[0] - 8)
    cut = (place == -1) | (place == 1023)
    uxs_ref[0] = jnp.zeros((80, 128), F32)

    def body(x):
        v = v_ref[x]
        above = v_ref[jnp.minimum(x + 1, 31)]
        uxs_ref[x + 1] = jnp.where(x == 31, 0.0, edge_weight(above - v))
        uy_ref[x] = jnp.where(lane == 127, 0.0, edge_weight(lanes(v, -1) - v))
        uz_ref[x] = jnp.where(cut, 0.0, edge_weight(rows(v, -1) - v))

    loop(32, body)
    even = lane_id((32, 128)) % 2 == 0

    def coarse(x):
        l1_ref[2, x] = pack_pair(
            plane_pair(uxs_ref, 2 * x + 2, False, False), plane_pair(uxs_ref, 2 * x + 18, False, False)
        )
        a, b = plane_pair(uy_ref, 2 * x, True, False), plane_pair(uy_ref, 2 * x + 16, True, False)
        l1_ref[3, x] = jnp.where(even, lanes(a, -1), b)
        l1_ref[4, x] = pack_pair(
            plane_pair(uz_ref, 2 * x, True, True), plane_pair(uz_ref, 2 * x + 16, True, True)
        )

    loop(8, coarse)
    copies.start(uxs_ref, uxs_hbm)
    copies.start(uy_ref, uy_hbm)
    copies.start(uz_ref, uz_hbm)
    for copy in arrived[3:]:
        copy.wait()
    label = lab_ref[0].astype(F32)

    def setup(x):
        seed = s_ref[x]
        f = jnp.where(seed == label, PENALTY, 0.0)
        source = jnp.where(seed >= 0.0, REACT + PENALTY, REACT)
        d = diagonal(source, uxs_ref, uy_ref, uz_ref, x, 1)
        di = OMEGA / d
        s_ref[x] = source
        f_ref[x] = f
        d_ref[x] = d
        di_ref[x] = di
        v_ref[x] = di * f

    loop(32, setup)
    copies.start(d_ref, d_hbm)
    copies.start(di_ref, di_hbm)
    copies.start(f_ref, f_hbm)
    restrict_fine(s_ref, l1_ref, 1)
    pre_relax(f_ref, v_ref, e_ref, s_ref, (uxs_ref, uy_ref, uz_ref, d_ref, di_ref), lambda: copies.start(e_ref, e_hbm))
    restrict_fine(s_ref, l1_ref, 0)
    copies.finish()


def add_coarse(e_ref, c_ref, o_ref, p_ref):
    even = lane_id((40, 128)) % 2 == 0

    def body(x):
        v = c_ref[x]
        for part in range(2):
            if part == 0:
                w = jnp.where(even, v, 0.0)
                w = w + lanes(w, 1)
            else:
                w = jnp.where(even, 0.0, v)
                w = w + lanes(w, -1)
            at = 2 * x + 16 * part
            slot = x % 4 + 4 * part
            p_ref[slot, pl.ds(0, 40, stride=2), :] = w
            p_ref[slot, pl.ds(1, 40, stride=2), :] = w
            wide = p_ref[slot]
            o_ref[at] = e_ref[at] + wide
            o_ref[at + 1] = e_ref[at + 1] + wide

    loop(8, body)


def post_relax(f_ref, a_ref, b_ref, level):
    uxs_ref, uy_ref, uz_ref, di_ref = level
    for src, dst in ((a_ref, b_ref), (b_ref, a_ref)):

        def sweep(x):
            v, total = neighbours(src, uxs_ref, uy_ref, uz_ref, x, 1, False)
            dst[x] = KEEP * v + di_ref[x] * (f_ref[x] + total)

        loop(32, sweep)


def middle_kernel(
    l1, ll, lr, f1, fl, fr, uxs_hbm, uy_hbm, uz_hbm, d_hbm, di_hbm, f_hbm, e_hbm,
    zq_hbm, q_hbm, e2_hbm, m1_ref, dots_ref,
    uxs_ref, uy_ref, uz_ref, d_ref, di_ref, f_ref, e_ref, zq_ref, q_ref, a_ref, b_ref, dots_acc, p_ref, c_ref, *rest,
):
    copies = Copies(rest[-1])
    load1(copies, (l1, ll, lr), (f1, fl, fr), rest)
    small, copies.open = copies.open, []
    for src, dst in ((e_hbm, e_ref), (uxs_hbm, uxs_ref), (uy_hbm, uy_ref), (uz_hbm, uz_ref), (di_hbm, di_ref),
                     (f_hbm, f_ref), (d_hbm, d_ref)):
        copies.start(src, dst)
    for copy in small:
        copy.wait()
    coarse_solve(c_ref, *rest[:-1])
    copies.finish()
    add_coarse(e_ref, c_ref, a_ref, p_ref)
    post_relax(f_ref, a_ref, b_ref, (uxs_ref, uy_ref, uz_ref, di_ref))
    spread(a_ref, zq_ref, 0, copies, zq_hbm)

    def image(x):
        v, total = neighbours(a_ref, uxs_ref, uy_ref, uz_ref, x, 1, False)
        q = d_ref[x] * v - total
        q_ref[x] = q
        b_ref[x] = di_ref[x] * q
        return (f_ref[x] * v)[8:72], (v * q)[8:72]

    dots_acc[...] = jnp.zeros_like(dots_acc)
    loop(32, image, acc=dots_acc)
    copies.start(q_ref, q_hbm)
    spread(q_ref, zq_ref, 1, copies, zq_hbm)
    pre_relax(
        q_ref, b_ref, e_ref, a_ref, (uxs_ref, uy_ref, uz_ref, d_ref, di_ref),
        lambda: copies.start(e_ref, e2_hbm), dots_acc,
    )
    restrict_fine(a_ref, m1_ref, 0)
    rz, pq, qw = jnp.sum(dots_acc[0]), jnp.sum(dots_acc[1]), jnp.sum(dots_acc[2])
    lane = lane_id((8, 128))
    dots_ref[...] = jnp.where(lane == 0, rz, jnp.where(lane == 1, pq, jnp.where(lane == 2, qw, 0.0)))
    copies.finish()


def last_kernel(
    lab_ref, l1, ll, lr, f1, fl, fr, uxs_hbm, uy_hbm, uz_hbm, di_hbm, q_hbm, e_hbm, dots_ref,
    wo_hbm, line_ref,
    uxs_ref, uy_ref, uz_ref, di_ref, q_ref, e_ref, wo_ref, a_ref, b_ref, p_ref, c_ref, *rest,
):
    copies = Copies(rest[-1])
    load1(copies, (l1, ll, lr), (f1, fl, fr), rest)
    small, copies.open = copies.open, []
    for src, dst in ((e_hbm, e_ref), (uxs_hbm, uxs_ref), (uy_hbm, uy_ref), (uz_hbm, uz_ref), (di_hbm, di_ref),
                     (q_hbm, q_ref)):
        copies.start(src, dst)
    for copy in small:
        copy.wait()
    energy = coarse_solve(c_ref, *rest[:-1])
    line = dots_ref[...] + jnp.where(lane_id((8, 128)) == 2, energy, 0.0)
    line_ref[...] = jnp.where(row_id((8, 128)) == lab_ref[0], line, 0.0)
    copies.finish()
    add_coarse(e_ref, c_ref, a_ref, p_ref)
    post_relax(q_ref, a_ref, b_ref, (uxs_ref, uy_ref, uz_ref, di_ref))
    spread(a_ref, wo_ref, 0, copies, wo_hbm)
    copies.finish()


def load1(copies, weights, target, scratch):
    ux1, uy1, uz1, f1, t1 = scratch[0], scratch[1], scratch[2], scratch[3], scratch[8]
    for (core, left, right), field, dst, at in (
        (weights, 2, ux1, 1), (weights, 3, uy1, 0), (weights, 4, uz1, 0), (weights, 1, t1, 0), (target, 0, f1, 0),
    ):
        for src, low, n in ((left, 0, 24), (core, 24, 32), (right, 56, 24)):
            copies.start(src.at[field], dst.at[pl.ds(at, 8), pl.ds(low, n)])


def pair1(v_ref, x, both_x, upper_z):
    total = v_ref[x, pl.ds(1, 40, stride=2), :]
    if not upper_z:
        total = total + v_ref[x, pl.ds(0, 40, stride=2), :]
    if both_x:
        total = total + pair1(v_ref, x + 1, False, upper_z)
    return total


def coarse_solve(
    o_ref, ux1, uy1, uz1, f1, d1, di1, v1, v1b, t1, ux2, uy2, uz2, f2, di2, v2, v2b, p_ref
):
    ux1[0] = lanes(ux1[8], 1)

    valid = lane_id((40, 128)) % 4 < 2

    def fold(v):
        return jnp.where(valid, v, 0.0)

    for x in range(4):
        a = pair1(ux1, 2 * x + 2, False, False)
        ux2[x + 1] = fold(a + lanes(a, -2))
        uy2[x] = fold(lanes(pair1(uy1, 2 * x, True, False), -2))
        a = pair1(uz1, 2 * x, True, True)
        uz2[x] = fold(a + lanes(a, -2))
    ux2[0] = lanes(ux2[4], 1)
    for x in range(4):
        a = pair1(t1, 2 * x, True, False)
        d = diagonal(fold(a + lanes(a, -2)), ux2, uy2, uz2, x, 4)
        di2[x] = jnp.where(d > 0.0, OMEGA / d, 0.0)

    def setup(x):
        d = diagonal(t1[x], ux1, uy1, uz1, x, 2)
        di = jnp.where(d > 0.0, OMEGA / d, 0.0)
        d1[x] = d
        di1[x] = di
        v1[x + 1] = di * f1[x]

    loop(8, setup)

    def relax1(src, dst):
        ghosts(src, 8)

        def sweep(x):
            v, total = neighbours(src, ux1, uy1, uz1, x, 2, True)
            dst[x + 1] = KEEP * v + di1[x] * (f1[x] + total)

        loop(8, sweep)

    relax1(v1, v1b)
    ghosts(v1b, 8)

    dot = jnp.zeros((32, 128), F32)
    for x in range(8):
        v, total = neighbours(v1b, ux1, uy1, uz1, x, 2, True)
        f = f1[x]
        r = f - d1[x] * v + total
        t1[x] = r
        dot = dot + (v * (f + r))[24:56]

    for x in range(4):
        a = pair1(t1, 2 * x, True, False)
        f2[x] = fold(a + lanes(a, -2))
        v2[x + 1] = di2[x] * f2[x]
    src, dst = v2, v2b
    for _ in range(COARSE_SWEEPS - 1):
        ghosts(src, 4)
        for x in range(4):
            v, total = neighbours(src, ux2, uy2, uz2, x, 4, True)
            dst[x + 1] = KEEP * v + di2[x] * (f2[x] + total)
        src, dst = dst, src

    low = row_id((40, 128))
    own = (low >= 12) & (low < 28)
    dot2 = jnp.zeros((40, 128), F32)
    for x in range(4):
        dot2 = dot2 + jnp.where(own, src[x + 1] * f2[x], 0.0)
    energy = jnp.sum(dot) + jnp.sum(dot2)

    for x in range(4):
        w = src[x + 1]
        w = w + lanes(w, 2)
        p_ref[x, pl.ds(0, 40, stride=2), :] = w
        p_ref[x, pl.ds(1, 40, stride=2), :] = w
        wide = p_ref[x]
        v1b[2 * x + 1] = v1b[2 * x + 1] + wide
        v1b[2 * x + 2] = v1b[2 * x + 2] + wide
    relax1(v1b, v1)
    relax1(v1, v1b)
    for x in range(8):
        o_ref[x] = v1b[x + 1, 20:60]
    return energy


def output_kernel(odd_ref, seed_ref, sums_ref, zq_ref, w_ref, sol_ref, res_ref, dir_ref):
    odd = odd_ref[0]
    everyone = jnp.sum(sums_ref[...], axis=0)
    low = lane_id((32, 128)) < 64
    for j in range(2):
        label = 2 * pl.program_id(0) + j
        sums = jnp.sum(jnp.where(row_id((8, 128)) == label, everyone, 0.0), axis=0, keepdims=True)
        rz, pq, qw = sums[:, 0:1], sums[:, 1:2], sums[:, 2:3]
        step = rz / pq
        more = (step * step * qw) / rz
        for x in range(4):
            pair = []
            for ref, at in ((zq_ref, x), (zq_ref, x + 4), (w_ref, x)):
                a, b = ref[2 * j + odd, 32 * at : 32 * at + 32], ref[2 * j + 1 - odd, 32 * at : 32 * at + 32]
                pair.append((jnp.where(low, a, lanes(b, 64)), jnp.where(low, lanes(a, 64), b)))
            for k in range(2):
                z, q, w = pair[0][k], pair[1][k], pair[2][k]
                at = x + 4 * k
                f = jnp.where(seed_ref[at] == label, PENALTY, 0.0)
                sol_ref[j, at] = step * z
                res_ref[j, at] = f - step * q
                dir_ref[j, at] = more * z - step * w


def sds(*shape):
    return jax.ShapeDtypeStruct(shape, F32)


def call(kernel, out, args, smem=0, vmem=0, scratch=(), sems=0, cost=1000000, name=None):
    here, scalar = pl.BlockSpec(memory_space=pltpu.VMEM), pl.BlockSpec(memory_space=pltpu.SMEM)
    away = pl.BlockSpec(memory_space=pl.ANY)
    args = list(args)
    for k in range(smem, len(args) - vmem):
        if args[k].shape in (FINE, TALL, (8, 32, 128)):
            args[k] = pltpu.with_memory_space_constraint(args[k], pltpu.HBM)
    return pl.pallas_call(
        kernel,
        out_shape=[pltpu.HBM(shape, F32) if far else sds(*shape) for shape, far in out],
        in_specs=[scalar] * smem + [away] * (len(args) - smem - vmem) + [here] * vmem,
        out_specs=[pl.BlockSpec(memory_space=pltpu.HBM) if far else here for _, far in out],
        scratch_shapes=[pltpu.VMEM(s, F32) if isinstance(s, tuple) else s for s in scratch] + ([pltpu.SemaphoreType.DMA((sems,))] if sems else []),
        compiler_params=pltpu.CompilerParams(vmem_limit_bytes=VLIMIT),
        cost_estimate=pl.CostEstimate(flops=cost, bytes_accessed=cost, transcendentals=0),
        name=name,
    )(*args)


FINE = (32, 80, 128)
TALL = (33, 80, 128)
LEVEL1 = (8, 80, 128)
LEVEL2 = (4, 40, 128)
COARSE = (
    [(9, 80, 128)] + [LEVEL1] * 5 + [(10, 80, 128)] * 2 + [LEVEL1]
    + [(5, 40, 128)] + [LEVEL2] * 4 + [(6, 40, 128)] * 2 + [(4, 80, 128)]
)


def z_chain():
    def at(label, gz, half):
        return (2 * label + (half ^ (gz & 1))) * 8 + gz

    pairs = []
    for label in range(LABELS):
        for gz in range(8):
            pairs.append((at(label, gz, 0), at(label, gz, 1)))
            if gz < 7:
                pairs.append((at(label, gz, 1), at(label, gz + 1, 0)))
    return pairs


def swap(first, last):
    every = ("gx", "gy", "gz")
    up = z_chain()
    down = [(b, a) for a, b in up]
    return lax.ppermute(last, every, up), lax.ppermute(first, every, down)


def swap1(v):
    return swap(v[:, :, 0:24], v[:, :, 8:32])


def local(intensity, seed_labels):
    gx, gy, gz = lax.axis_index("gx"), lax.axis_index("gy"), lax.axis_index("gz")
    group = ("gx", "gy")
    odd = (gz & 1).reshape(1)
    half = (gy ^ gz) & 1
    label = ((4 * gx + gy) // 2).reshape(1)
    z_base = (128 * gz + 64 * half).reshape(1)

    sent = call(
        pack_kernel, [((16, 8, 32, 128), False)], (odd, intensity, seed_labels), smem=1,
        scratch=[(8, 32, 128), pltpu.VMEM((8, 32, 128), jnp.int32)], sems=2, name="pack",
    )[0]
    got = lax.all_to_all(sent, group, 0, 0, tiled=True)
    core, first, last = call(
        assemble_kernel,
        [((64, 64, 128), False), ((64, 8, 128), False), ((64, 8, 128), False)],
        (got,),
        vmem=1,
        name="turn",
    )
    left, right = swap(first, last)
    uxs, uy, uz, d, di, f, e, l1 = call(
        first_kernel,
        [(TALL, True)] + [(FINE, True)] * 6 + [((5, 8, 32, 128), False)],
        (z_base, label, core, left, right),
        smem=2,
        scratch=[TALL] + [FINE] * 8,
        sems=13,
        name="first",
    )
    ll, lr = swap1(l1)
    zq, q, e2, m1, dots = call(
        middle_kernel,
        [((16, 256, 128), True), (FINE, True), (FINE, True), ((1, 8, 32, 128), False), ((8, 128), False)],
        (l1, ll, lr, l1, ll, lr, uxs, uy, uz, d, di, f, e),
        scratch=[TALL] + [FINE] * 6 + [(16, 256, 128)] + [FINE] * 3 + [(3, 64, 128), (8, 80, 128), (8, 40, 128)] + COARSE,
        sems=32,
        name="middle",
    )
    ml, mr = swap1(m1)
    zq, ml, mr = lax.optimization_barrier((zq, ml, mr))
    zqr = lax.all_to_all(zq, group, 0, 0, tiled=True)
    wo, line = call(
        last_kernel,
        [((16, 136, 128), True), ((8, 128), False)],
        (label, l1, ll, lr, m1, ml, mr, uxs, uy, uz, di, q, e2, dots),
        smem=1,
        vmem=1,
        scratch=[TALL] + [FINE] * 5 + [(16, 128, 128)] + [FINE] * 2 + [(8, 80, 128), (8, 40, 128)] + COARSE,
        sems=25,
        name="last",
    )
    sums = lax.psum(line, "gz")
    wo, zqr = lax.optimization_barrier((wo, zqr))
    wo = lax.dynamic_update_slice(wo, jnp.broadcast_to(sums, (16, 8, 128)), (0, 128, 0))
    wr_ = lax.all_to_all(wo, group, 0, 0, tiled=True)

    return tuple(
        pl.pallas_call(
            output_kernel,
            grid=(LABELS // 2,),
            out_shape=[sds(8, 8, 32, 128)] * 3,
            in_specs=[
                pl.BlockSpec(memory_space=pltpu.SMEM),
                pl.BlockSpec((8, 32, 128), lambda i: (0, 0, 0)),
                pl.BlockSpec((16, 8, 128), lambda i: (0, 16, 0)),
                pl.BlockSpec((4, 256, 128), lambda i: (i, 0, 0)),
                pl.BlockSpec((4, 136, 128), lambda i: (i, 0, 0)),
            ],
            out_specs=[pl.BlockSpec((2, 8, 32, 128), lambda i: (i, 0, 0, 0))] * 3,
            compiler_params=pltpu.CompilerParams(vmem_limit_bytes=VLIMIT),
            name="output",
        )(odd, seed_labels, wr_, zqr, wr_)
    )


def solution(mesh):
    placed = (P("gx", "gy", "gz"), P("gx", "gy", "gz"))
    return jax.shard_map(
        local,
        mesh=mesh,
        in_specs=placed,
        out_specs=(P(None, "gx", "gy", "gz"), P(None, "gx", "gy", "gz"), P(None, "gx", "gy", "gz")),
        check_vma=False,
    )
```
